512 devices in a mesh: grp: 32 (over x, y), dev: 16 (over z, core).
Axes of the slice: x: 4, y: 8, z: 8, core: 2. Of those that a mesh axis runs over, the one named last changes fastest.
Arguments:
- prompt_latent_cache: bfloat16 [64, 4096, 512], P('grp', 'dev'), may hold values from -6 to 6
- prompt_rope: bfloat16 [64, 64, 4096], P('grp', None, 'dev'), may hold values from -32 to 32
- prompt_length: int32 [32, 2], P('grp'), may hold values from 256 to 4096, as said below
- dest_slot: int32 [32, 2], P('grp'), may hold values from 0 to 63, as said below
- resident_latent: bfloat16 [64, 4096, 512], P('grp', 'dev'), may hold values from -6 to 6
- resident_rope: bfloat16 [64, 64, 4096], P('grp', None, 'dev'), may hold values from -32 to 32
- resident_length: int32 [32, 2], P('grp'), may hold values from 256 to 4096, as said below
- new_latent: bfloat16 [128, 2, 512], P('grp'), may hold values from -6 to 6
- new_rope: bfloat16 [128, 2, 64], P('grp'), may hold values from -32 to 32
- query_nope: bfloat16 [128, 2, 128, 128], P('grp', None, 'dev'), may hold values from -6 to 6
- query_rope: bfloat16 [128, 2, 128, 64], P('grp', None, 'dev'), may hold values from -64 to 64
- key_up: bfloat16 [128, 128, 512], P('dev'), may hold values from -0.5 to 0.5
- value_up_weight: bfloat16 [128, 512, 128], P('dev'), may hold values from -0.25 to 0.25
Outputs:
- per_head_output: bfloat16 [128, 2, 128, 128], P('grp', None, 'dev')
The draws below stay inside these ranges and needn't reach their ends.
Inputs may be any that keep to these rules, and one draw needn't show every extreme that they name: dest_slot[g, r] = q * 2 + c sends prompt r of prefill group g to slot c (below 2) of decode group q. All entries differ, the prompts of one prefill group go to different decode groups, and every decode group receives exactly 2 prompts. `prompt_length`: in every prefill group some prompt has exactly 4096 tokens. `resident_length`: in every decode group some resident request has exactly 4096 tokens.
All inputs are finite; a program needn't handle non-finite values.
Results may differ from the reference program's by a relative error of at most 0.0084.
Values may be sent and summed in bfloat16 or wider, within the bound.
A program may use at most 64 MiB of HBM per device.

```python
import math
import jax
import jax.numpy as jnp
from jax import lax

H = 128
DN = 128
DR = 64
KV_RANK = 512
DV = 128
REQ = 2
RES = 2
STEPS = 2
TOKS_DEV = 256
LEN = 4096
CAP = 2
SLOTS = 4
ALL_REQ = 64
ALL_RES = 64
ALL_SLOTS = 128
N_GRP = 32


def slot_keys(key):
    return 1.5 * jax.random.normal(jax.random.fold_in(key, 101), (ALL_SLOTS, STEPS, DR), jnp.float32)


def ragged_lengths(key, groups, count):
    key_full, key_rest = jax.random.split(key, 2)
    full_place = jax.random.randint(key_full, (groups,), 0, count).astype(jnp.int32)
    others = jax.random.randint(key_rest, (groups, count), LEN // 16, LEN + 1).astype(jnp.int32)
    places = jnp.arange(count, dtype=jnp.int32)
    return jnp.where(places[None, :] == full_place[:, None], LEN, others).astype(jnp.int32)


def draw_prompt_length(key, part):
    key = jax.random.fold_in(key, 11)
    return ragged_lengths(key, N_GRP, REQ)


def draw_resident_length(key, part):
    key = jax.random.fold_in(key, 12)
    return ragged_lengths(key, N_GRP, RES)


def draw_query_rope(key, part):
    shared = slot_keys(key)
    key = jax.random.fold_in(key, 3)
    key_gain, key_noise = jax.random.split(key, 2)
    head_gain = jnp.exp(jax.random.uniform(key_gain, (H,), jnp.float32, math.log(0.52), math.log(0.67)))
    values = head_gain[None, None, :, None] * shared[:, :, None, :]
    values = values + 0.5 * jax.random.normal(key_noise, (ALL_SLOTS, STEPS, H, DR), jnp.float32)
    return jnp.clip(values, -64.0, 64.0).astype(jnp.bfloat16)


def draw_new_rope(key, part):
    shared = slot_keys(key)
    key = jax.random.fold_in(key, 4)
    values = shared + 0.5 * jax.random.normal(key, (ALL_SLOTS, STEPS, DR), jnp.float32)
    return jnp.clip(values, -32.0, 32.0).astype(jnp.bfloat16)


def draw_prompt_rope(key, part):
    key = jax.random.fold_in(key, 5)
    values = jax.random.normal(key, (ALL_REQ, DR, LEN), jnp.float32)
    return jnp.clip(values, -32.0, 32.0).astype(jnp.bfloat16)


def draw_resident_rope(key, part):
    key = jax.random.fold_in(key, 6)
    values = jax.random.normal(key, (ALL_RES, DR, LEN), jnp.float32)
    return jnp.clip(values, -32.0, 32.0).astype(jnp.bfloat16)


def draw_dest_slot(key, part):
    key = jax.random.fold_in(key, 9)
    key_outer, key_inner, key_offset, key_slots = jax.random.split(key, 4)
    outer = jax.random.permutation(key_outer, N_GRP).astype(jnp.int32)
    inner = jax.random.permutation(key_inner, N_GRP).astype(jnp.int32)
    offsets = jax.random.permutation(key_offset, N_GRP).astype(jnp.int32)[:REQ]
    placed = (inner[:, None] + offsets[None, :]) % N_GRP
    flat_target = outer[placed].reshape(-1)
    matches = (flat_target[:, None] == jnp.arange(N_GRP, dtype=jnp.int32)[None, :]).astype(jnp.int32)
    before = jnp.cumsum(matches, axis=0) - matches
    rank_in = jnp.sum(before * matches, axis=1)
    tables = jax.vmap(lambda slot_key: jax.random.permutation(slot_key, CAP).astype(jnp.int32))(jax.random.split(key_slots, N_GRP))
    slot_index = tables[flat_target, rank_in]
    return (flat_target * CAP + slot_index).reshape(N_GRP, REQ).astype(jnp.int32)


def level_of(stream_key, extent, cuts, low, largest):
    factor_of = 1.0
    for axis_at, shards_of in cuts:
        heights = jax.random.uniform(jax.random.fold_in(jax.random.fold_in(stream_key, 6), axis_at), (shards_of,), jnp.float32, low / len(cuts), largest / len(cuts))
        factor_of = factor_of * jnp.repeat(jnp.exp(heights), extent[axis_at] // shards_of).reshape((-1,) + (1,) * (len(extent) - 1 - axis_at))
    return factor_of


def centred(stream_key, extent, spread, limit, cuts=(), kind=jnp.bfloat16):
    gain = level_of(stream_key, extent, cuts, -0.22, 0.18) if cuts else 1.0
    array = jax.random.normal(stream_key, extent, jnp.float32) * spread * gain
    return jnp.minimum(jnp.maximum(array, -limit), limit).astype(kind)


def setup_inputs(seed: int = 0) -> dict:
    keys = jax.random.split(jax.random.key(seed), 14)
    prompt_latent_cache = centred(keys[0], (ALL_REQ, LEN, KV_RANK), 1.0, 6.0, ((0, 32), (1, 16)))
    prompt_rope = draw_prompt_rope(jax.random.fold_in(keys[13], 71), 0)
    prompt_length = draw_prompt_length(jax.random.fold_in(keys[13], 71), 0)
    dest_slot = draw_dest_slot(jax.random.fold_in(keys[13], 71), 0)
    resident_latent = centred(keys[4], (ALL_RES, LEN, KV_RANK), 1.0, 6.0, ((0, 32), (1, 16)))
    resident_rope = draw_resident_rope(jax.random.fold_in(keys[13], 71), 0)
    resident_length = draw_resident_length(jax.random.fold_in(keys[13], 71), 0)
    new_latent = centred(keys[7], (ALL_SLOTS, STEPS, KV_RANK), 1.0, 6.0, ((0, 32),))
    new_rope = draw_new_rope(jax.random.fold_in(keys[13], 71), 0)
    query_nope = centred(keys[9], (ALL_SLOTS, STEPS, H, DN), 1.0, 6.0, ((0, 32), (2, 16)))
    query_rope = draw_query_rope(jax.random.fold_in(keys[13], 71), 0)
    key_up = centred(keys[11], (H, DN, KV_RANK), DN ** -0.5, 0.5, ((0, 16),))
    value_up_weight = centred(keys[12], (H, KV_RANK, DV), KV_RANK ** -0.5, 0.25, ((0, 16),))
    return {"prompt_latent_cache": prompt_latent_cache, "prompt_rope": prompt_rope, "prompt_length": prompt_length, "dest_slot": dest_slot, "resident_latent": resident_latent, "resident_rope": resident_rope, "resident_length": resident_length, "new_latent": new_latent, "new_rope": new_rope, "query_nope": query_nope, "query_rope": query_rope, "key_up": key_up, "value_up_weight": value_up_weight}


def attend_scale():
    return (0.1 * math.log(40.0) + 1.0) ** 2 / math.sqrt(DN + DR)

def reference(prompt_latent_cache, prompt_rope, prompt_length, dest_slot, resident_latent, resident_rope, resident_length, new_latent, new_rope, query_nope, query_rope, key_up, value_up_weight):
    score_scale = attend_scale()
    flat_dest = dest_slot.reshape(-1).astype(jnp.int32)
    request_of_slot = jnp.zeros((N_GRP * CAP,), jnp.int32).at[flat_dest].set(jnp.arange(ALL_REQ, dtype=jnp.int32) + 1) - 1
    flat_len = prompt_length.reshape(-1).astype(jnp.int32)
    res_len = resident_length.reshape(-1).astype(jnp.int32)
    key_wide = key_up.astype(jnp.float32)
    expanded_value = value_up_weight.astype(jnp.float32)
    step_ids = jnp.arange(STEPS, dtype=jnp.int32)
    causal = step_ids[:, None] >= step_ids[None, :]
    blocks = LEN // TOKS_DEV

    def one_slot(slot_id):
        decode_group = slot_id // SLOTS
        slot_inner = slot_id % SLOTS
        is_res = slot_inner < RES
        res_row = decode_group * RES + jnp.minimum(slot_inner, RES - 1)
        request = request_of_slot[decode_group * CAP + jnp.maximum(slot_inner - RES, 0)]
        has_request = request >= 0
        req_row = jnp.maximum(request, 0)
        latent = jnp.where(is_res, resident_latent[res_row], prompt_latent_cache[req_row]).astype(jnp.float32)
        rotary = jnp.where(is_res, resident_rope[res_row], prompt_rope[req_row]).astype(jnp.float32)
        length = jnp.where(is_res, res_len[res_row], jnp.where(has_request, flat_len[req_row], 0))
        absorbed = jnp.einsum('thn,hnk->thk', query_nope[slot_id].astype(jnp.float32), key_wide)
        absorbed = lax.optimization_barrier(absorbed.astype(jnp.bfloat16)).astype(jnp.float32)
        rotary_query = query_rope[slot_id].astype(jnp.float32)
        scores = score_scale * (jnp.einsum('thk,pk->thp', absorbed, latent) + jnp.einsum('thr,rp->thp', rotary_query, rotary))
        scores = scores.reshape(STEPS, H, blocks, TOKS_DEV)
        is_live = (jnp.arange(LEN, dtype=jnp.int32) < length).reshape(blocks, TOKS_DEV)
        masked = jnp.where(is_live, scores, -1e+30)
        block_max = lax.optimization_barrier(jnp.max(masked, axis=-1))
        weights = jnp.where(is_live, jnp.exp(masked - block_max[..., None]), 0.0)
        block_total = lax.optimization_barrier(jnp.sum(weights, axis=-1))
        rounded = lax.optimization_barrier(weights.astype(jnp.bfloat16)).astype(jnp.float32)
        summed = jnp.einsum('thbp,bpk->thbk', rounded, latent.reshape(blocks, TOKS_DEV, KV_RANK))
        block_out = (summed / jnp.maximum(block_total, 1.0)[..., None]).astype(jnp.bfloat16)
        block_out = lax.optimization_barrier(block_out).astype(jnp.float32)
        fresh_latent = new_latent[slot_id].astype(jnp.float32)
        fresh_rotary = new_rope[slot_id].astype(jnp.float32)
        new_scores = score_scale * (jnp.einsum('thk,nk->thn', absorbed, fresh_latent) + jnp.einsum('thr,nr->thn', rotary_query, fresh_rotary))
        new_masked = jnp.where(causal[:, None, :], new_scores, -1e+30)
        row_top = jnp.maximum(lax.optimization_barrier(jnp.max(block_max, axis=-1)), lax.optimization_barrier(jnp.max(new_masked, axis=-1)))
        block_weight = block_total * jnp.exp(block_max - row_top[..., None])
        new_weight = jnp.where(causal[:, None, :], jnp.exp(new_masked - row_top[..., None]), 0.0)
        numerator = jnp.einsum('thb,thbk->thk', block_weight, block_out) + jnp.einsum('thn,nk->thk', new_weight, fresh_latent)
        denominator = lax.optimization_barrier(jnp.sum(block_weight, axis=-1)) + lax.optimization_barrier(jnp.sum(new_weight, axis=-1))
        attention_result = lax.optimization_barrier((numerator / denominator[..., None]).astype(jnp.bfloat16)).astype(jnp.float32)
        return jnp.einsum('roc,ocj->roj', attention_result, expanded_value).astype(jnp.bfloat16)
    return lax.map(one_slot, jnp.arange(ALL_SLOTS, dtype=jnp.int32))
```

```python
import functools
import math

import jax
import jax.numpy as jnp
from jax import lax
from jax.experimental import pallas as pl
from jax.experimental.pallas import tpu as pltpu
from jax.sharding import PartitionSpec as P

MESH = pl.DeviceIdType.MESH
F32 = jnp.float32
BF16 = jnp.bfloat16
NX, NY, NZ = 4, 8, 8
NG = NX * NY
NEG = -1e30


def attend_scale(nope_width, rotary_width):
    return (0.1 * math.log(40.0) + 1.0) ** 2 / math.sqrt(nope_width + rotary_width)


def iota(shape, axis):
    return lax.broadcasted_iota(jnp.int32, shape, axis)


def columns_of(rows, field):
    n = rows.shape[0]
    hit = iota((n, 16, 128), 2) == iota((n, 16, 128), 1) + 16 * field
    return jnp.sum(jnp.where(hit, jnp.broadcast_to(rows, (n, 16, 128)), 0.0), axis=-1, keepdims=True)


def rows_of(fields):
    n = fields[0].shape[0]
    lane, sub = iota((n, 16, 128), 2), iota((n, 16, 128), 1)
    packed = jnp.zeros((n, 16, 128), F32)
    for f, column in enumerate(fields):
        packed = jnp.where(lane == sub + 16 * f, jnp.broadcast_to(column, (n, 16, 128)), packed)
    return jnp.sum(packed, axis=1, keepdims=True)


def absorb(q32, kup):
    head = iota((32, 512), 0) % 8
    total = jnp.zeros((32, 512), F32)
    for h in range(8):
        total = jnp.where(head == h, jnp.dot(q32, kup[h], preferred_element_type=F32), total)
    return total.astype(BF16)


def new_scores(scale, absorbed, ropes, fresh, fresh_rope):
    step = iota((16, 1), 0) // 8
    out = []
    for s in range(2):
        q = absorbed[s * 16 : (s + 1) * 16].astype(F32)
        pair = []
        for n in range(2):
            v = jnp.sum(q * fresh[s][n], axis=-1, keepdims=True)
            v = v + jnp.sum(ropes[s] * fresh_rope[s][n], axis=-1, keepdims=True)
            v = v * scale
            pair.append(v if n == 0 else jnp.where(step >= 1, v, NEG))
        out.append(pair)
    return out


def attend(scale, gathered, latent, rope, lengths, offset, out_bf, out_st):
    ropes = gathered[:, 128:144, :].reshape(256, 128)
    position = offset + iota((256, 256), 1)
    blank = jnp.zeros((64, 256), BF16)
    fields = [None] * 4
    for s in range(2):
        q = jnp.concatenate(
            [gathered[:, k * 32 + s * 16 : k * 32 + s * 16 + 16, :].reshape(256, 128) for k in range(4)],
            axis=1,
        )
        keys = latent[s]
        rk = jnp.concatenate([rope[s], blank] if s == 0 else [blank, rope[s]], axis=0)
        scores = lax.dot_general(q, keys, (((1,), (1,)), ((), ())), preferred_element_type=F32)
        scores = scale * (scores + jnp.dot(ropes, rk, preferred_element_type=F32))
        live = position < lengths[s]
        scores = jnp.where(live, scores, NEG)
        top = jnp.max(scores, axis=-1, keepdims=True)
        weights = jnp.where(live, jnp.exp(scores - top), 0.0)
        total = jnp.sum(weights, axis=-1, keepdims=True)
        summed = jnp.dot(weights.astype(BF16), keys, preferred_element_type=F32)
        summed = summed / jnp.maximum(total, 1.0)
        out_bf[:, s * 16 : (s + 1) * 16, :] = summed.reshape(16, 16, 512).astype(BF16)
        fields[s] = top.reshape(16, 16, 1)
        fields[2 + s] = total.reshape(16, 16, 1)
    out_st[...] = rows_of(fields)


def merge_cores(own_bf, own_st, other_bf, other_st, out_bf, out_st):
    fields = [None] * 4
    for s in range(2):
        m1, l1 = columns_of(own_st, s), columns_of(own_st, 2 + s)
        m2, l2 = columns_of(other_st[...], s), columns_of(other_st[...], 2 + s)
        top = jnp.maximum(m1, m2)
        a, b = l1 * jnp.exp(m1 - top), l2 * jnp.exp(m2 - top)
        total = a + b
        under = 1.0 / jnp.maximum(total, 1.0)
        rows = slice(s * 16, (s + 1) * 16)
        o = own_bf(rows).astype(F32) * (a * under) + other_bf[:, rows, :].astype(F32) * (b * under)
        out_bf[:, rows, :] = o.astype(BF16)
        fields[s], fields[2 + s] = top, total
    out_st[...] = rows_of(fields)


def finish(blocks, stats, fresh_scores, fresh, vup):
    rows = []
    for s in range(2):
        m, l = columns_of(stats[...], s), columns_of(stats[...], 2 + s)
        n0, n1 = fresh_scores[s]
        top = jnp.maximum(jnp.max(m, axis=0), jnp.maximum(n0, n1))
        w = l * jnp.exp(m - top[None])
        w0 = jnp.exp(n0 - top)
        w1 = jnp.where(n1 > NEG, jnp.exp(n1 - top), 0.0)
        under = jnp.sum(w, axis=0) + w0 + w1
        total = w0 * fresh[s][0] + w1 * fresh[s][1]
        for j in range(NZ):
            total = total + w[j] * blocks[j, s * 16 : (s + 1) * 16, :].astype(F32)
        rows.append(total / under)
    attended = jnp.concatenate(rows, axis=0).astype(BF16)
    head = iota((32, 128), 0) % 8
    out = jnp.zeros((32, 128), F32)
    for h in range(8):
        out = jnp.where(head == h, jnp.dot(attended, vup[h], preferred_element_type=F32), out)
    return out


def kernel(
    scale,
    plat_hbm, prope, plen, dest, rlat_hbm, rrope, rlen, nlat, nrope, qn, qr, kup_hbm, vup_hbm,
    out,
    plat, rlat, kup, vup, aux, pay, xsend, xrecv, g_res, g_inc,
    obf, ost, sib_bf, sib_st, zs_bf, zs_st, zr_bf, zr_st, ret_send, ret_recv, small,
    load_sem, aux_ss, aux_rs, y_ss, y_rs, x_ss, x_rs, gz_ss, gz_rs, gs_ss, gs_rs,
    cs_ss, cs_rs, zo_ss, zo_rs, zt_ss, zt_rs, ret_ss, ret_rs,
):
    g, d = lax.axis_index("grp"), lax.axis_index("dev")
    x, y = g // NY, g % NY
    z, c = d // 2, d % 2
    mine = c * NZ + z
    sibling = (g, z * 2 + 1 - c)

    loads = [
        pltpu.make_async_copy(src, dst, load_sem.at[i])
        for i, (src, dst) in enumerate(
            [(kup_hbm, kup), (rlat_hbm, rlat), (plat_hbm, plat), (vup_hbm, vup)]
        )
    ]
    for load in loads:
        load.start()

    barrier = pltpu.get_barrier_semaphore()

    def greet(k, _):
        pl.semaphore_signal(barrier, inc=1, device_id=((g + k) % NG, d), device_id_type=MESH)
        return 0

    lax.fori_loop(1, NG, greet, 0)
    for k in range(1, NZ):
        pl.semaphore_signal(barrier, inc=1, device_id=(g, ((z + k) % NZ) * 2 + c), device_id_type=MESH)
    pl.semaphore_signal(barrier, inc=1, device_id=sibling, device_id_type=MESH)

    def remote(src, dst, ss, rs, device):
        return pltpu.make_async_remote_copy(
            src_ref=src, dst_ref=dst, send_sem=ss, recv_sem=rs, device_id=device, device_id_type=MESH
        )

    qn_all = qn[...].astype(F32).reshape(64, 128)
    qr_all = qr[...].astype(F32).reshape(64, 64)
    fresh_all = nlat[...].astype(F32)
    fresh_rope_all = nrope[...].astype(F32)
    for i in range(2):
        s = 2 + i
        for n in range(2):
            for k in range(4):
                small[n * 4 + k : n * 4 + k + 1, :] = fresh_all[s, n : n + 1, k * 128 : (k + 1) * 128]
        rope_rows = jnp.concatenate(
            [qr_all[s * 16 : s * 16 + 8], qr_all[s * 16 + 8 : s * 16 + 16]], axis=1
        )
        payload = jnp.concatenate([qn_all[s * 16 : (s + 1) * 16], rope_rows, small[...]], axis=0)
        pay[y, i] = payload.astype(BF16)
        aux[g * 2 + i, 0:1, :] = jnp.full((1, 128), dest[0, i].astype(F32))
        aux[g * 2 + i, 1:2, :] = jnp.concatenate(
            [fresh_rope_all[s, 0:1], fresh_rope_all[s, 1:2]], axis=1
        )

    pl.semaphore_wait(barrier, NG - 1 + NZ - 1 + 1)

    def y_copy(to, frm):
        return remote(pay.at[y], pay.at[y], y_ss.at[to], y_rs.at[frm], (x * NY + to, d))

    for k in range(1, NY):
        y_copy((y + k) % NY, y).start()

    def aux_copy(to, frm):
        ref = aux.at[pl.ds(g * 2, 2)]
        return remote(ref, ref, aux_ss.at[to], aux_rs.at[frm], (to, d))

    def send_aux(k, _):
        aux_copy((g + k) % NG, g).start()
        return 0

    lax.fori_loop(1, NG, send_aux, 0)

    def gather_start(p, gathered, absorbed, ropes):
        for k in range(4):
            gathered[mine, k * 32 : (k + 1) * 32, :] = absorbed[:, k * 128 : (k + 1) * 128]
        gathered[mine, 128:144, :] = jnp.concatenate(ropes, axis=1).astype(BF16)
        for k in range(1, NZ):
            to = (z + k) % NZ
            gather_z(p, gathered, to, z).start()
        gather_sib(p, gathered, z).start()

    def gather_z(p, gathered, to, frm):
        ref = gathered.at[mine]
        return remote(ref, ref, gz_ss.at[p, to], gz_rs.at[p, frm], (g, to * 2 + c))

    def gather_sib(p, gathered, frm):
        ref = gathered.at[c * NZ + frm]
        return remote(ref, ref, gs_ss.at[p, frm], gs_rs.at[p, frm], sibling)

    def gather_forward(p, gathered):
        for k in (1, 7, 2, 6, 3, 5, 4):
            frm = (z + k) % NZ
            gather_z(p, gathered, frm, frm).wait_recv()
            gather_sib(p, gathered, frm).start()

    def gather_finish(p, gathered):
        for frm in range(NZ):
            gather_sib(p, gathered, frm).wait_recv()

    loads[0].wait()
    absorbed_res = absorb(qn_all[0:32].astype(BF16), kup)
    ropes_res = [qr_all[0:16], qr_all[16:32]]
    gather_start(0, g_res, absorbed_res, ropes_res)
    fresh_res = [[fresh_all[s, n : n + 1] for n in range(2)] for s in range(2)]
    fresh_rope_res = [[fresh_rope_all[s, n : n + 1] for n in range(2)] for s in range(2)]
    scores_res = new_scores(scale, absorbed_res, ropes_res, fresh_res, fresh_rope_res)

    for k in range(1, NY):
        frm = (y + k) % NY
        y_copy(frm, frm).wait_recv()

    def wait_aux(k, _):
        frm = (g + k) % NG
        aux_copy(frm, frm).wait_recv()
        return 0

    lax.fori_loop(1, NG, wait_aux, 0)

    def x_copy(to, frm):
        return remote(xsend.at[to], xrecv.at[x], x_ss.at[to], x_rs.at[frm], (to * NY + y, d))

    for k in (1, 2, 3, 0):
        to = (x + k) % NX
        for r in range(2):
            wanted = aux[(to * NY + y) * 2 + r, 0:1, :]
            block = jnp.zeros((32, 128), F32)
            for j in range(NY):
                for i in range(2):
                    here = ((x * NY + j) * 2 + i).astype(F32)
                    hit = jnp.broadcast_to(wanted == here, (32, 128))
                    block = jnp.where(hit, pay[j, i].astype(F32), block)
            if k:
                xsend[to, r] = block.astype(BF16)
            else:
                xrecv[x, r] = block.astype(BF16)
        if k:
            x_copy(to, x).start()

    gather_forward(0, g_res)

    for k in range(1, NX):
        frm = (x + k) % NX
        x_copy(frm, frm).wait_recv()
    queries, ropes_inc, fresh_inc, fresh_rope_inc = [], [], [], []
    for r in range(2):
        block = xrecv[0, r].astype(F32)
        for j in range(1, NX):
            block = block + xrecv[j, r].astype(F32)
        queries.append(block[0:16])
        ropes_inc.append(jnp.concatenate([block[16:24, 0:64], block[16:24, 64:128]], axis=0))
        small[...] = block[24:32]
        fresh_inc.append(
            [
                jnp.concatenate([small[n * 4 + k : n * 4 + k + 1, :] for k in range(4)], axis=1)
                for n in range(2)
            ]
        )
        row = aux[dest[0, r], 1:2, :]
        fresh_rope_inc.append([row[:, 0:64], row[:, 64:128]])
    absorbed_inc = absorb(jnp.concatenate(queries, axis=0).astype(BF16), kup)
    gather_start(1, g_inc, absorbed_inc, ropes_inc)
    scores_inc = new_scores(scale, absorbed_inc, ropes_inc, fresh_inc, fresh_rope_inc)

    offset = d * 256

    def cores_copy(p):
        half = pl.ds((1 - c) * NZ, NZ)
        return (
            remote(obf.at[p, half], sib_bf.at[p], cs_ss.at[p, 0], cs_rs.at[p, 0], sibling),
            remote(ost.at[p, half], sib_st.at[p], cs_ss.at[p, 1], cs_rs.at[p, 1], sibling),
        )

    def out_copy(p, to, frm):
        device = (g, to * 2 + c)
        return (
            remote(zs_bf.at[p, to], zr_bf.at[p, z], zo_ss.at[p, to], zo_rs.at[p, frm], device),
            remote(zs_st.at[p, to], zr_st.at[p, z], zt_ss.at[p, to], zt_rs.at[p, frm], device),
        )

    def partials(p, gathered, latent, rope, lengths):
        attend(scale, gathered, latent, rope, lengths, offset, obf.at[p], ost.at[p])
        for copy in cores_copy(p):
            copy.start()

    def exchange(p):
        for copy in cores_copy(p):
            copy.wait_recv()
        own = pl.ds(c * NZ, NZ)
        merge_cores(
            lambda rows: obf[p, own, rows, :], ost[p, own], sib_bf.at[p], sib_st.at[p],
            zs_bf.at[p], zs_st.at[p],
        )
        for k in (4, 3, 5, 2, 6, 1, 7):
            for copy in out_copy(p, (z + k) % NZ, z):
                copy.start()
        zr_bf[p, z] = zs_bf[p, z]
        zr_st[p, z] = zs_st[p, z]

    def collect(p):
        for k in range(1, NZ):
            frm = (z + k) % NZ
            for copy in out_copy(p, frm, frm):
                copy.wait_recv()

    gather_finish(0, g_res)
    loads[1].wait()
    partials(0, g_res, rlat, rrope, [rlen[0, 0], rlen[0, 1]])
    gather_forward(1, g_inc)
    exchange(0)
    gather_finish(1, g_inc)
    loads[2].wait()
    partials(1, g_inc, plat, prope, [plen[0, 0], plen[0, 1]])
    exchange(1)

    loads[3].wait()
    collect(0)
    out_res = finish(zr_bf.at[0], zr_st.at[0], scores_res, fresh_res, vup)
    out[0:2] = out_res.reshape(2, 2, 8, 128).astype(BF16)

    collect(1)
    out_inc = finish(zr_bf.at[1], zr_st.at[1], scores_inc, fresh_inc, vup)

    def ret_block(to):
        block = jnp.zeros((16, 128), F32)
        for r in range(2):
            goal = aux[g * 2 + r, 0:1, :]
            first = (to * 2).astype(F32)
            hit = (goal == first) | (goal == first + 1.0)
            block = jnp.where(jnp.broadcast_to(hit, (16, 128)), out_inc[r * 16 : (r + 1) * 16], block)
        return block.astype(BF16)

    def ret_copy(to, frm):
        return remote(ret_send.at[to], ret_recv.at[g], ret_ss.at[to], ret_rs.at[frm], (to, d))

    def ret_start(k, _):
        to = (g + k) % NG
        ret_send[to] = ret_block(to)
        ret_copy(to, g).start()
        return 0

    lax.fori_loop(1, NG, ret_start, 0)
    ret_recv[g] = ret_block(g)

    def ret_wait(k, _):
        frm = (g + k) % NG
        ret_copy(frm, frm).wait_recv()
        return 0

    lax.fori_loop(1, NG, ret_wait, 0)

    def choose(frm, chosen):
        block = ret_recv[frm].astype(F32)
        picked = []
        for i in range(2):
            here = (g * 2 + i).astype(F32)
            hit = (aux[frm * 2, 0:1, :] == here) | (aux[frm * 2 + 1, 0:1, :] == here)
            picked.append(jnp.where(jnp.broadcast_to(hit, (16, 128)), block, chosen[i]))
        return tuple(picked)

    zero = jnp.zeros((16, 128), F32)
    chosen = lax.fori_loop(0, NG, choose, (zero, zero))
    for i in range(2):
        out[2 + i] = chosen[i].reshape(2, 8, 128).astype(BF16)

    def drain(k, _):
        to = (g + k) % NG
        aux_copy(to, g).wait_send()
        ret_copy(to, g).wait_send()
        return 0

    lax.fori_loop(1, NG, drain, 0)
    for k in range(1, NY):
        y_copy((y + k) % NY, y).wait_send()
    for k in range(1, NX):
        x_copy((x + k) % NX, x).wait_send()
    for p, gathered in ((0, g_res), (1, g_inc)):
        for k in range(1, NZ):
            to = (z + k) % NZ
            gather_z(p, gathered, to, z).wait_send()
            for copy in out_copy(p, to, z):
                copy.wait_send()
        for frm in range(NZ):
            gather_sib(p, gathered, frm).wait_send()
        for copy in cores_copy(p):
            copy.wait_send()


def body(
    prompt_latent_cache, prompt_rope, prompt_length, dest_slot, resident_latent, resident_rope,
    resident_length, new_latent, new_rope, query_nope, query_rope, key_up, value_up_weight,
):
    scale = attend_scale(query_nope.shape[-1], query_rope.shape[-1])
    vmem = pl.BlockSpec(memory_space=pltpu.VMEM)
    smem = pl.BlockSpec(memory_space=pltpu.SMEM)
    hbm = pl.BlockSpec(memory_space=pl.ANY)
    dma = pltpu.SemaphoreType.DMA
    return pl.pallas_call(
        functools.partial(kernel, scale),
        out_shape=jax.ShapeDtypeStruct((4, 2, 8, 128), BF16),
        in_specs=[hbm, vmem, smem, smem, hbm, vmem, smem, vmem, vmem, vmem, vmem, hbm, hbm],
        out_specs=vmem,
        scratch_shapes=[
            pltpu.VMEM((2, 256, 512), BF16),
            pltpu.VMEM((2, 256, 512), BF16),
            pltpu.VMEM((8, 128, 512), BF16),
            pltpu.VMEM((8, 512, 128), BF16),
            pltpu.VMEM((NG * 2, 2, 128), F32),
            pltpu.VMEM((NY, 2, 32, 128), BF16),
            pltpu.VMEM((NX, 2, 32, 128), BF16),
            pltpu.VMEM((NX, 2, 32, 128), BF16),
            pltpu.VMEM((16, 144, 128), BF16),
            pltpu.VMEM((16, 144, 128), BF16),
            pltpu.VMEM((2, 16, 32, 512), BF16),
            pltpu.VMEM((2, 16, 1, 128), F32),
            pltpu.VMEM((2, NZ, 32, 512), BF16),
            pltpu.VMEM((2, NZ, 1, 128), F32),
            pltpu.VMEM((2, NZ, 32, 512), BF16),
            pltpu.VMEM((2, NZ, 1, 128), F32),
            pltpu.VMEM((2, NZ, 32, 512), BF16),
            pltpu.VMEM((2, NZ, 1, 128), F32),
            pltpu.VMEM((NG, 16, 128), BF16),
            pltpu.VMEM((NG, 16, 128), BF16),
            pltpu.VMEM((8, 128), F32),
            dma((4,)),
            dma((NG,)), dma((NG,)),
            dma((NY,)), dma((NY,)),
            dma((NX,)), dma((NX,)),
            dma((2, NZ)), dma((2, NZ)),
            dma((2, NZ)), dma((2, NZ)),
            dma((2, 2)), dma((2, 2)),
            dma((2, NZ)), dma((2, NZ)),
            dma((2, NZ)), dma((2, NZ)),
            dma((NG,)), dma((NG,)),
        ],
        compiler_params=pltpu.CompilerParams(
            collective_id=0, has_side_effects=True, vmem_limit_bytes=48 << 20
        ),
        name="latent_attend",
    )(
        prompt_latent_cache, prompt_rope, prompt_length, dest_slot, resident_latent, resident_rope,
        resident_length, new_latent, new_rope, query_nope, query_rope, key_up, value_up_weight,
    )


def solution(mesh):
    placed = (
        P("grp", "dev", None),
        P("grp", None, "dev"),
        P("grp", None),
        P("grp", None),
        P("grp", "dev", None),
        P("grp", None, "dev"),
        P("grp", None),
        P("grp", None, None),
        P("grp", None, None),
        P("grp", None, "dev", None),
        P("grp", None, "dev", None),
        P("dev", None, None),
        P("dev", None, None),
    )
    return jax.shard_map(
        body, mesh=mesh, in_specs=placed, out_specs=P("grp", None, "dev", None), check_vma=False
    )
```

```python
import functools
import math

import jax
import jax.numpy as jnp
from jax import lax
from jax.experimental import pallas as pl
from jax.experimental.pallas import tpu as pltpu
from jax.sharding import PartitionSpec as P

MESH = pl.DeviceIdType.MESH
F32 = jnp.float32
BF16 = jnp.bfloat16
NX, NY, NZ = 4, 8, 8
NG = NX * NY
NEG = -1e30


def attend_scale(nope_width, rotary_width):
    return (0.1 * math.log(40.0) + 1.0) ** 2 / math.sqrt(nope_width + rotary_width)


def iota(shape, axis):
    return lax.broadcasted_iota(jnp.int32, shape, axis)


def columns_of(rows, field):
    n = rows.shape[0]
    hit = iota((n, 16, 128), 2) == iota((n, 16, 128), 1) + 16 * field
    return jnp.sum(jnp.where(hit, jnp.broadcast_to(rows, (n, 16, 128)), 0.0), axis=-1, keepdims=True)


def rows_of(fields):
    n = fields[0].shape[0]
    lane, sub = iota((n, 16, 128), 2), iota((n, 16, 128), 1)
    packed = jnp.zeros((n, 16, 128), F32)
    for f, column in enumerate(fields):
        packed = jnp.where(lane == sub + 16 * f, jnp.broadcast_to(column, (n, 16, 128)), packed)
    return jnp.sum(packed, axis=1, keepdims=True)


def absorb(q32, kup):
    head = iota((32, 512), 0) % 8
    total = jnp.zeros((32, 512), F32)
    for h in range(8):
        total = jnp.where(head == h, jnp.dot(q32, kup[h], preferred_element_type=F32), total)
    return total.astype(BF16)


def new_scores(scale, absorbed, ropes, fresh, fresh_rope):
    step = iota((16, 1), 0) // 8
    out = []
    for s in range(2):
        q = absorbed[s * 16 : (s + 1) * 16].astype(F32)
        pair = []
        for n in range(2):
            v = jnp.sum(q * fresh[s][n], axis=-1, keepdims=True)
            v = v + jnp.sum(ropes[s] * fresh_rope[s][n], axis=-1, keepdims=True)
            v = v * scale
            pair.append(v if n == 0 else jnp.where(step >= 1, v, NEG))
        out.append(pair)
    return out


def attend(scale, gathered, latent, rope, lengths, offset, out_bf, out_st):
    ropes = gathered[:, 128:144, :].reshape(256, 128)
    position = offset + iota((256, 256), 1)
    blank = jnp.zeros((64, 256), BF16)
    fields = [None] * 4
    for s in range(2):
        q = jnp.concatenate(
            [gathered[:, k * 32 + s * 16 : k * 32 + s * 16 + 16, :].reshape(256, 128) for k in range(4)],
            axis=1,
        )
        keys = latent[s]
        rk = jnp.concatenate([rope[s], blank] if s == 0 else [blank, rope[s]], axis=0)
        scores = lax.dot_general(q, keys, (((1,), (1,)), ((), ())), preferred_element_type=F32)
        scores = scale * (scores + jnp.dot(ropes, rk, preferred_element_type=F32))
        live = position < lengths[s]
        scores = jnp.where(live, scores, NEG)
        top = jnp.max(scores, axis=-1, keepdims=True)
        weights = jnp.where(live, jnp.exp(scores - top), 0.0)
        total = jnp.sum(weights, axis=-1, keepdims=True)
        summed = jnp.dot(weights.astype(BF16), keys, preferred_element_type=F32)
        summed = summed / jnp.maximum(total, 1.0)
        out_bf[:, s * 16 : (s + 1) * 16, :] = summed.reshape(16, 16, 512).astype(BF16)
        fields[s] = top.reshape(16, 16, 1)
        fields[2 + s] = total.reshape(16, 16, 1)
    out_st[...] = rows_of(fields)


def merge_cores(own_bf, own_st, other_bf, other_st, out_bf, out_st):
    fields = [None] * 4
    for s in range(2):
        m1, l1 = columns_of(own_st, s), columns_of(own_st, 2 + s)
        m2, l2 = columns_of(other_st[...], s), columns_of(other_st[...], 2 + s)
        top = jnp.maximum(m1, m2)
        a, b = l1 * jnp.exp(m1 - top), l2 * jnp.exp(m2 - top)
        total = a + b
        under = 1.0 / jnp.maximum(total, 1.0)
        rows = slice(s * 16, (s + 1) * 16)
        o = own_bf(rows).astype(F32) * (a * under) + other_bf[:, rows, :].astype(F32) * (b * under)
        out_bf[:, rows, :] = o.astype(BF16)
        fields[s], fields[2 + s] = top, total
    out_st[...] = rows_of(fields)


def finish(blocks, stats, fresh_scores, fresh, vup):
    rows = []
    for s in range(2):
        m, l = columns_of(stats[...], s), columns_of(stats[...], 2 + s)
        n0, n1 = fresh_scores[s]
        top = jnp.maximum(jnp.max(m, axis=0), jnp.maximum(n0, n1))
        w = l * jnp.exp(m - top[None])
        w0 = jnp.exp(n0 - top)
        w1 = jnp.where(n1 > NEG, jnp.exp(n1 - top), 0.0)
        under = jnp.sum(w, axis=0) + w0 + w1
        total = w0 * fresh[s][0] + w1 * fresh[s][1]
        for j in range(NZ):
            total = total + w[j] * blocks[j, s * 16 : (s + 1) * 16, :].astype(F32)
        rows.append(total / under)
    attended = jnp.concatenate(rows, axis=0).astype(BF16)
    head = iota((32, 128), 0) % 8
    out = jnp.zeros((32, 128), F32)
    for h in range(8):
        out = jnp.where(head == h, jnp.dot(attended, vup[h], preferred_element_type=F32), out)
    return out


def kernel(
    scale,
    plat_hbm, prope_hbm, plen_hbm, dest_hbm, rlat_hbm, rrope_hbm, rlen_hbm, nlat_hbm, nrope_hbm,
    qn_hbm, qr_hbm, kup_hbm, vup_hbm,
    out,
    plat, prope, plen, dest, rlat, rrope, rlen, nlat, nrope, qn, qr, kup, vup, aux, pay, xsend, xrecv, g_res, g_inc,
    obf, ost, sib_bf, sib_st, zs_bf, zs_st, zr_bf, zr_st, ret_send, ret_recv, small,
    load_sem, aux_ss, aux_rs, y_ss, y_rs, x_ss, x_rs, gz_ss, gz_rs, gs_ss, gs_rs,
    cs_ss, cs_rs, zo_ss, zo_rs, zt_ss, zt_rs, ret_ss, ret_rs,
):
    g, d = lax.axis_index("grp"), lax.axis_index("dev")
    x, y = g // NY, g % NY
    z, c = d // 2, d % 2
    mine = c * NZ + z
    sibling = (g, z * 2 + 1 - c)

    loads = [
        pltpu.make_async_copy(src, dst, load_sem.at[i])
        for i, (src, dst) in enumerate(
            [
                (qn_hbm, qn), (qr_hbm, qr), (nlat_hbm, nlat), (nrope_hbm, nrope), (dest_hbm, dest),
                (kup_hbm, kup),
                (rlat_hbm, rlat), (rrope_hbm, rrope), (rlen_hbm, rlen),
                (plat_hbm, plat), (prope_hbm, prope), (plen_hbm, plen),
                (vup_hbm, vup),
            ]
        )
    ]
    need_small, need_kup, need_res, need_inc, need_vup = (
        loads[0:5], loads[5:6], loads[6:9], loads[9:12], loads[12:13]
    )

    waiting = list(loads)

    def arrive(wanted):
        for load in wanted:
            load.wait()
            waiting.remove(load)

    sent = []

    def send(copy):
        copy.start()
        sent.append(copy)

    def over_groups(start):
        def step(k, _):
            start((g + k) % NG)
            return 0

        lax.fori_loop(1, NG, step, 0)

    sent_over_groups = []

    def drain():
        for load in waiting:
            load.wait()
        for copy in sent:
            copy.wait_send()
        if sent_over_groups:
            over_groups(lambda to: [copy(to, g).wait_send() for copy in sent_over_groups])

    for load in loads:
        load.start()

    barrier = pltpu.get_barrier_semaphore()

    def greet(k, _):
        pl.semaphore_signal(barrier, inc=1, device_id=((g + k) % NG, d), device_id_type=MESH)
        return 0

    lax.fori_loop(1, NG, greet, 0)
    for k in range(1, NZ):
        pl.semaphore_signal(barrier, inc=1, device_id=(g, ((z + k) % NZ) * 2 + c), device_id_type=MESH)
    pl.semaphore_signal(barrier, inc=1, device_id=sibling, device_id_type=MESH)

    def remote(src, dst, ss, rs, device):
        return pltpu.make_async_remote_copy(
            src_ref=src, dst_ref=dst, send_sem=ss, recv_sem=rs, device_id=device, device_id_type=MESH
        )

    arrive(need_small)
    qn_all = qn[...].astype(F32).reshape(64, 128)
    qr_all = qr[...].astype(F32).reshape(64, 64)
    fresh_all = nlat[...].astype(F32)
    fresh_rope_all = nrope[...].astype(F32)
    for i in range(2):
        s = 2 + i
        for n in range(2):
            for k in range(4):
                small[n * 4 + k : n * 4 + k + 1, :] = fresh_all[s, n : n + 1, k * 128 : (k + 1) * 128]
        rope_rows = jnp.concatenate(
            [qr_all[s * 16 : s * 16 + 8], qr_all[s * 16 + 8 : s * 16 + 16]], axis=1
        )
        payload = jnp.concatenate([qn_all[s * 16 : (s + 1) * 16], rope_rows, small[...]], axis=0)
        pay[y, i] = payload.astype(BF16)
        aux[g * 2 + i, 0:1, :] = jnp.full((1, 128), dest[0, i].astype(F32))
        aux[g * 2 + i, 1:2, :] = jnp.concatenate(
            [fresh_rope_all[s, 0:1], fresh_rope_all[s, 1:2]], axis=1
        )

    pl.semaphore_wait(barrier, NG - 1 + NZ - 1 + 1)

    def y_copy(to, frm):
        return remote(pay.at[y], pay.at[y], y_ss.at[to], y_rs.at[frm], (x * NY + to, d))

    for k in range(1, NY):
        send(y_copy((y + k) % NY, y))

    def aux_copy(to, frm):
        ref = aux.at[pl.ds(g * 2, 2)]
        return remote(ref, ref, aux_ss.at[to], aux_rs.at[frm], (to, d))

    over_groups(lambda to: aux_copy(to, g).start())
    sent_over_groups.append(aux_copy)

    def gather_start(p, gathered, absorbed, ropes):
        for k in range(4):
            gathered[mine, k * 32 : (k + 1) * 32, :] = absorbed[:, k * 128 : (k + 1) * 128]
        gathered[mine, 128:144, :] = jnp.concatenate(ropes, axis=1).astype(BF16)
        for k in range(1, NZ):
            to = (z + k) % NZ
            send(gather_z(p, gathered, to, z))
        send(gather_sib(p, gathered, z))

    def gather_z(p, gathered, to, frm):
        ref = gathered.at[mine]
        return remote(ref, ref, gz_ss.at[p, to], gz_rs.at[p, frm], (g, to * 2 + c))

    def gather_sib(p, gathered, frm):
        ref = gathered.at[c * NZ + frm]
        return remote(ref, ref, gs_ss.at[p, frm], gs_rs.at[p, frm], sibling)

    def gather_forward(p, gathered):
        for k in (1, 7, 2, 6, 3, 5, 4):
            frm = (z + k) % NZ
            gather_z(p, gathered, frm, frm).wait_recv()
            send(gather_sib(p, gathered, frm))

    def gather_finish(p, gathered):
        for frm in range(NZ):
            gather_sib(p, gathered, frm).wait_recv()

    arrive(need_kup)
    absorbed_res = absorb(qn_all[0:32].astype(BF16), kup)
    ropes_res = [qr_all[0:16], qr_all[16:32]]
    gather_start(0, g_res, absorbed_res, ropes_res)
    fresh_res = [[fresh_all[s, n : n + 1] for n in range(2)] for s in range(2)]
    fresh_rope_res = [[fresh_rope_all[s, n : n + 1] for n in range(2)] for s in range(2)]
    scores_res = new_scores(scale, absorbed_res, ropes_res, fresh_res, fresh_rope_res)

    for k in range(1, NY):
        frm = (y + k) % NY
        y_copy(frm, frm).wait_recv()

    over_groups(lambda frm: aux_copy(frm, frm).wait_recv())

    def x_copy(to, frm):
        return remote(xsend.at[to], xrecv.at[x], x_ss.at[to], x_rs.at[frm], (to * NY + y, d))

    for k in (1, 2, 3, 0):
        to = (x + k) % NX
        for r in range(2):
            wanted = aux[(to * NY + y) * 2 + r, 0:1, :]
            block = jnp.zeros((32, 128), F32)
            for j in range(NY):
                for i in range(2):
                    here = ((x * NY + j) * 2 + i).astype(F32)
                    hit = jnp.broadcast_to(wanted == here, (32, 128))
                    block = jnp.where(hit, pay[j, i].astype(F32), block)
            if k:
                xsend[to, r] = block.astype(BF16)
            else:
                xrecv[x, r] = block.astype(BF16)
        if k:
            send(x_copy(to, x))

    gather_forward(0, g_res)

    for k in range(1, NX):
        frm = (x + k) % NX
        x_copy(frm, frm).wait_recv()
    queries, ropes_inc, fresh_inc, fresh_rope_inc = [], [], [], []
    for r in range(2):
        block = xrecv[0, r].astype(F32)
        for j in range(1, NX):
            block = block + xrecv[j, r].astype(F32)
        queries.append(block[0:16])
        ropes_inc.append(jnp.concatenate([block[16:24, 0:64], block[16:24, 64:128]], axis=0))
        small[...] = block[24:32]
        fresh_inc.append(
            [
                jnp.concatenate([small[n * 4 + k : n * 4 + k + 1, :] for k in range(4)], axis=1)
                for n in range(2)
            ]
        )
        row = aux[dest[0, r], 1:2, :]
        fresh_rope_inc.append([row[:, 0:64], row[:, 64:128]])
    absorbed_inc = absorb(jnp.concatenate(queries, axis=0).astype(BF16), kup)
    gather_start(1, g_inc, absorbed_inc, ropes_inc)
    scores_inc = new_scores(scale, absorbed_inc, ropes_inc, fresh_inc, fresh_rope_inc)

    offset = d * 256

    def cores_copy(p):
        half = pl.ds((1 - c) * NZ, NZ)
        return (
            remote(obf.at[p, half], sib_bf.at[p], cs_ss.at[p, 0], cs_rs.at[p, 0], sibling),
            remote(ost.at[p, half], sib_st.at[p], cs_ss.at[p, 1], cs_rs.at[p, 1], sibling),
        )

    def out_copy(p, to, frm):
        device = (g, to * 2 + c)
        return (
            remote(zs_bf.at[p, to], zr_bf.at[p, z], zo_ss.at[p, to], zo_rs.at[p, frm], device),
            remote(zs_st.at[p, to], zr_st.at[p, z], zt_ss.at[p, to], zt_rs.at[p, frm], device),
        )

    def partials(p, gathered, latent, rope, lengths):
        attend(scale, gathered, latent, rope, lengths, offset, obf.at[p], ost.at[p])
        for copy in cores_copy(p):
            send(copy)

    def exchange(p):
        for copy in cores_copy(p):
            copy.wait_recv()
        own = pl.ds(c * NZ, NZ)
        merge_cores(
            lambda rows: obf[p, own, rows, :], ost[p, own], sib_bf.at[p], sib_st.at[p],
            zs_bf.at[p], zs_st.at[p],
        )
        for k in (4, 3, 5, 2, 6, 1, 7):
            for copy in out_copy(p, (z + k) % NZ, z):
                send(copy)
        zr_bf[p, z] = zs_bf[p, z]
        zr_st[p, z] = zs_st[p, z]

    def collect(p):
        for k in range(1, NZ):
            frm = (z + k) % NZ
            for copy in out_copy(p, frm, frm):
                copy.wait_recv()

    gather_finish(0, g_res)
    arrive(need_res)
    partials(0, g_res, rlat, rrope, [rlen[0, 0], rlen[0, 1]])
    gather_forward(1, g_inc)
    exchange(0)
    gather_finish(1, g_inc)
    arrive(need_inc)
    partials(1, g_inc, plat, prope, [plen[0, 0], plen[0, 1]])
    exchange(1)

    arrive(need_vup)
    collect(0)
    out_res = finish(zr_bf.at[0], zr_st.at[0], scores_res, fresh_res, vup)
    out[0:2] = out_res.reshape(2, 2, 8, 128).astype(BF16)

    collect(1)
    out_inc = finish(zr_bf.at[1], zr_st.at[1], scores_inc, fresh_inc, vup)

    def ret_block(to):
        block = jnp.zeros((16, 128), F32)
        for r in range(2):
            goal = aux[g * 2 + r, 0:1, :]
            first = (to * 2).astype(F32)
            hit = (goal == first) | (goal == first + 1.0)
            block = jnp.where(jnp.broadcast_to(hit, (16, 128)), out_inc[r * 16 : (r + 1) * 16], block)
        return block.astype(BF16)

    def ret_copy(to, frm):
        return remote(ret_send.at[to], ret_recv.at[g], ret_ss.at[to], ret_rs.at[frm], (to, d))

    def ret_start(to):
        ret_send[to] = ret_block(to)
        ret_copy(to, g).start()

    over_groups(ret_start)
    sent_over_groups.append(ret_copy)
    ret_recv[g] = ret_block(g)

    over_groups(lambda frm: ret_copy(frm, frm).wait_recv())

    def choose(frm, chosen):
        block = ret_recv[frm].astype(F32)
        picked = []
        for i in range(2):
            here = (g * 2 + i).astype(F32)
            hit = (aux[frm * 2, 0:1, :] == here) | (aux[frm * 2 + 1, 0:1, :] == here)
            picked.append(jnp.where(jnp.broadcast_to(hit, (16, 128)), block, chosen[i]))
        return tuple(picked)

    zero = jnp.zeros((16, 128), F32)
    chosen = lax.fori_loop(0, NG, choose, (zero, zero))
    for i in range(2):
        out[2 + i] = chosen[i].reshape(2, 8, 128).astype(BF16)

    drain()


def body(
    prompt_latent_cache, prompt_rope, prompt_length, dest_slot, resident_latent, resident_rope,
    resident_length, new_latent, new_rope, query_nope, query_rope, key_up, value_up_weight,
):
    scale = attend_scale(query_nope.shape[-1], query_rope.shape[-1])
    vmem = pl.BlockSpec(memory_space=pltpu.VMEM)
    hbm = pl.BlockSpec(memory_space=pltpu.HBM)
    dma = pltpu.SemaphoreType.DMA
    return pl.pallas_call(
        functools.partial(kernel, scale),
        out_shape=jax.ShapeDtypeStruct((4, 2, 8, 128), BF16),
        in_specs=[hbm] * 13,
        out_specs=vmem,
        scratch_shapes=[
            pltpu.VMEM((2, 256, 512), BF16),
            pltpu.VMEM((2, 64, 256), BF16),
            pltpu.SMEM((1, 2), jnp.int32),
            pltpu.SMEM((1, 2), jnp.int32),
            pltpu.VMEM((2, 256, 512), BF16),
            pltpu.VMEM((2, 64, 256), BF16),
            pltpu.SMEM((1, 2), jnp.int32),
            pltpu.VMEM((4, 2, 512), BF16),
            pltpu.VMEM((4, 2, 64), BF16),
            pltpu.VMEM((4, 2, 8, 128), BF16),
            pltpu.VMEM((4, 2, 8, 64), BF16),
            pltpu.VMEM((8, 128, 512), BF16),
            pltpu.VMEM((8, 512, 128), BF16),
            pltpu.VMEM((NG * 2, 2, 128), F32),
            pltpu.VMEM((NY, 2, 32, 128), BF16),
            pltpu.VMEM((NX, 2, 32, 128), BF16),
            pltpu.VMEM((NX, 2, 32, 128), BF16),
            pltpu.VMEM((16, 144, 128), BF16),
            pltpu.VMEM((16, 144, 128), BF16),
            pltpu.VMEM((2, 16, 32, 512), BF16),
            pltpu.VMEM((2, 16, 1, 128), F32),
            pltpu.VMEM((2, NZ, 32, 512), BF16),
            pltpu.VMEM((2, NZ, 1, 128), F32),
            pltpu.VMEM((2, NZ, 32, 512), BF16),
            pltpu.VMEM((2, NZ, 1, 128), F32),
            pltpu.VMEM((2, NZ, 32, 512), BF16),
            pltpu.VMEM((2, NZ, 1, 128), F32),
            pltpu.VMEM((NG, 16, 128), BF16),
            pltpu.VMEM((NG, 16, 128), BF16),
            pltpu.VMEM((8, 128), F32),
            dma((13,)),
            dma((NG,)), dma((NG,)),
            dma((NY,)), dma((NY,)),
            dma((NX,)), dma((NX,)),
            dma((2, NZ)), dma((2, NZ)),
            dma((2, NZ)), dma((2, NZ)),
            dma((2, 2)), dma((2, 2)),
            dma((2, NZ)), dma((2, NZ)),
            dma((2, NZ)), dma((2, NZ)),
            dma((NG,)), dma((NG,)),
        ],
        compiler_params=pltpu.CompilerParams(
            collective_id=0, has_side_effects=True, vmem_limit_bytes=48 << 20
        ),
        name="latent_attend",
    )(*(pltpu.with_memory_space_constraint(a, pltpu.HBM) for a in (
        prompt_latent_cache, prompt_rope, prompt_length, dest_slot, resident_latent, resident_rope,
        resident_length, new_latent, new_rope, query_nope, query_rope, key_up, value_up_weight,
    )))


def solution(mesh):
    placed = (
        P("grp", "dev", None),
        P("grp", None, "dev"),
        P("grp", None),
        P("grp", None),
        P("grp", "dev", None),
        P("grp", None, "dev"),
        P("grp", None),
        P("grp", None, None),
        P("grp", None, None),
        P("grp", None, "dev", None),
        P("grp", None, "dev", None),
        P("dev", None, None),
        P("dev", None, None),
    )
    return jax.shard_map(
        body, mesh=mesh, in_specs=placed, out_specs=P("grp", None, "dev", None), check_vma=False
    )
```

```python
import functools
import math

import jax
import jax.numpy as jnp
from jax import lax
from jax.experimental import pallas as pl
from jax.experimental.pallas import tpu as pltpu
from jax.sharding import PartitionSpec as P

MESH = pl.DeviceIdType.MESH
F32 = jnp.float32
BF16 = jnp.bfloat16
NX, NY, NZ = 4, 8, 8
NG = NX * NY
NEG = -1e30


def attend_scale(nope_width, rotary_width):
    return (0.1 * math.log(40.0) + 1.0) ** 2 / math.sqrt(nope_width + rotary_width)


def iota(shape, axis):
    return lax.broadcasted_iota(jnp.int32, shape, axis)


def columns_of(rows, field):
    n = rows.shape[0]
    hit = iota((n, 16, 128), 2) == iota((n, 16, 128), 1) + 16 * field
    return jnp.sum(jnp.where(hit, jnp.broadcast_to(rows, (n, 16, 128)), 0.0), axis=-1, keepdims=True)


def rows_of(fields):
    n = fields[0].shape[0]
    lane, sub = iota((n, 16, 128), 2), iota((n, 16, 128), 1)
    packed = jnp.zeros((n, 16, 128), F32)
    for f, column in enumerate(fields):
        packed = jnp.where(lane == sub + 16 * f, jnp.broadcast_to(column, (n, 16, 128)), packed)
    return jnp.sum(packed, axis=1, keepdims=True)


def absorb(q32, kup):
    head = iota((32, 512), 0) % 8
    total = jnp.zeros((32, 512), F32)
    for h in range(8):
        total = jnp.where(head == h, jnp.dot(q32, kup[h], preferred_element_type=F32), total)
    return total.astype(BF16)


def new_scores(scale, absorbed, ropes, fresh, fresh_rope):
    step = iota((16, 1), 0) // 8
    out = []
    for s in range(2):
        q = absorbed[s * 16 : (s + 1) * 16].astype(F32)
        pair = []
        for n in range(2):
            v = jnp.sum(q * fresh[s][n], axis=-1, keepdims=True)
            v = v + jnp.sum(ropes[s] * fresh_rope[s][n], axis=-1, keepdims=True)
            v = v * scale
            pair.append(v if n == 0 else jnp.where(step >= 1, v, NEG))
        out.append(pair)
    return out


def attend(scale, gathered, keys, rope, length, offset, out_bf):
    q = jnp.concatenate(
        [gathered[:, k * 16 : (k + 1) * 16, :].reshape(128, 128) for k in range(4)], axis=1
    )
    ropes = gathered[:, 64:80, :].reshape(128, 128)[:, 0:64]
    scores = lax.dot_general(q, keys, (((1,), (1,)), ((), ())), preferred_element_type=F32)
    scores = scale * (scores + jnp.dot(ropes, rope, preferred_element_type=F32))
    live = offset + iota((128, 512), 1) < length
    scores = jnp.where(live, scores, NEG)
    top = jnp.max(scores, axis=-1, keepdims=True)
    weights = jnp.where(live, jnp.exp(scores - top), 0.0)
    total = jnp.sum(weights, axis=-1, keepdims=True)
    summed = jnp.dot(weights.astype(BF16), keys, preferred_element_type=F32)
    summed = summed / jnp.maximum(total, 1.0)
    out_bf[...] = summed.reshape(8, 16, 512).astype(BF16)
    return top.reshape(8, 16, 1), total.reshape(8, 16, 1)


def finish(blocks, stats, fresh_scores, fresh, vup):
    rows = []
    for s in range(2):
        m, l = columns_of(stats[...], s), columns_of(stats[...], 2 + s)
        n0, n1 = fresh_scores[s]
        top = jnp.maximum(jnp.max(m, axis=0), jnp.maximum(n0, n1))
        w = l * jnp.exp(m - top[None])
        w0 = jnp.exp(n0 - top)
        w1 = jnp.where(n1 > NEG, jnp.exp(n1 - top), 0.0)
        under = jnp.sum(w, axis=0) + w0 + w1
        total = w0 * fresh[s][0] + w1 * fresh[s][1]
        for j in range(NZ):
            total = total + w[j] * blocks[s, j].astype(F32)
        rows.append(total / under)
    attended = jnp.concatenate(rows, axis=0).astype(BF16)
    head = iota((32, 128), 0) % 8
    out = jnp.zeros((32, 128), F32)
    for h in range(8):
        out = jnp.where(head == h, jnp.dot(attended, vup[h], preferred_element_type=F32), out)
    return out


def kernel(
    scale,
    plat_hbm, prope_hbm, plen_hbm, dest_hbm, rlat_hbm, rrope_hbm, rlen_hbm, nlat_hbm, nrope_hbm,
    qn_hbm, qr_hbm, kup_hbm, vup_hbm,
    out,
    lat, rope, plen, dest, rlen, nlat, nrope, qn, qr, kup, vup,
    dest_x, dest_all, pay_a, pay_b, xs_a, xs_b, xr_a, xr_b, gathered,
    zs_bf, zs_st, zr_bf, zr_st, ret_send, ret_recv, small,
    load_sem, sib_ss, sib_rs, ya_ss, ya_rs, yb_ss, yb_rs, xa_ss, xa_rs, xb_ss, xb_rs,
    dx_ss, dx_rs, da_ss, da_rs, gz_ss, gz_rs, zo_ss, zo_rs, zt_ss, zt_rs, ret_ss, ret_rs,
):
    g, d = lax.axis_index("grp"), lax.axis_index("dev")
    x, y = g // NY, g % NY
    z, c = d // 2, d % 2

    def along_z(k):
        return (g, ((z + k + NZ) % NZ) * 2 + c)

    def along_y(k):
        return (x * NY + (y + k) % NY, d)

    def along_x(k):
        return (((x + k) % NX) * NY + y, d)

    sibling = (g, z * 2 + 1 - c)

    barrier = pltpu.get_barrier_semaphore()
    peers = [along_y(k) for k in range(1, NY)] + [along_x(k) for k in range(1, NX)]
    peers += [sibling] + [along_z(k) for k in range(1, NZ)]
    for peer in peers:
        pl.semaphore_signal(barrier, inc=1, device_id=peer, device_id_type=MESH)

    half = pl.ds(pl.multiple_of(c * 256, 256), 256)
    loads = [
        pltpu.make_async_copy(src, dst, load_sem.at[i])
        for i, (src, dst) in enumerate(
            [
                (qn_hbm, qn), (qr_hbm, qr), (nlat_hbm, nlat), (nrope_hbm, nrope), (dest_hbm, dest),
                (kup_hbm, kup),
                (rlat_hbm, lat.at[0, :, half, :]), (rrope_hbm, rope.at[0, :, :, half]), (rlen_hbm, rlen),
                (plat_hbm, lat.at[1, :, half, :]), (prope_hbm, rope.at[1, :, :, half]), (plen_hbm, plen),
                (vup_hbm, vup),
            ]
        )
    ]
    need_small, need_kup, need_res, need_inc, need_vup = (
        loads[0:5], loads[5:6], loads[6:9], loads[9:12], loads[12:13]
    )
    for load in loads:
        load.start()
    waiting = list(loads)

    def arrive(wanted):
        for load in wanted:
            load.wait()
            waiting.remove(load)

    sent = []

    def send(copy):
        copy.start()
        sent.append(copy)

    def over_groups(start):
        def step(k, _):
            start((g + k) % NG)
            return 0

        lax.fori_loop(1, NG, step, 0)

    sent_over_groups = []

    def drain():
        for load in waiting:
            load.wait()
        for copy in sent:
            copy.wait_send()
        if sent_over_groups:
            over_groups(lambda to: [copy(to, g).wait_send() for copy in sent_over_groups])

    def remote(src, dst, ss, rs, device):
        return pltpu.make_async_remote_copy(
            src_ref=src, dst_ref=dst, send_sem=ss, recv_sem=rs, device_id=device, device_id_type=MESH
        )

    def sib_copies(p):
        lat_hbm, rope_hbm = ((rlat_hbm, rrope_hbm), (plat_hbm, prope_hbm))[p]
        return (
            remote(lat_hbm, lat.at[p, :, half, :], sib_ss.at[p, 0], sib_rs.at[p, 0], sibling),
            remote(rope_hbm, rope.at[p, :, :, half], sib_ss.at[p, 1], sib_rs.at[p, 1], sibling),
        )

    arrive(need_small)
    qn_all = qn[...].astype(F32).reshape(64, 128)
    qr_all = qr[...].astype(F32).reshape(64, 64)
    fresh_all = nlat[...].astype(F32)
    fresh_rope_all = nrope[...].astype(F32)
    rope_rows = [
        jnp.concatenate([qr_all[s * 16 : s * 16 + 8], qr_all[s * 16 + 8 : s * 16 + 16]], axis=1)
        for s in (2, 3)
    ]
    pay_a[y] = jnp.concatenate([qn_all[32:64]] + rope_rows, axis=0).astype(BF16)
    for i in range(2):
        dest_x[x * 2 + i] = jnp.full((1, 128), dest[0, i].astype(F32))
        dest_all[g * 2 + i] = jnp.full((1, 128), dest[0, i].astype(F32))

    pl.semaphore_wait(barrier, len(peers))

    def ya_copy(to, frm):
        return remote(pay_a.at[y], pay_a.at[y], ya_ss.at[to], ya_rs.at[frm], (x * NY + to, d))

    def yb_copy(to, frm):
        return remote(pay_b.at[y], pay_b.at[y], yb_ss.at[to], yb_rs.at[frm], (x * NY + to, d))

    def dx_copy(to, frm):
        ref = dest_x.at[pl.ds(x * 2, 2)]
        return remote(ref, ref, dx_ss.at[to], dx_rs.at[frm], (to * NY + y, d))

    for k in (4, 3, 5, 2, 6, 1, 7):
        send(ya_copy((y + k) % NY, y))
    for k in range(1, NX):
        send(dx_copy((x + k) % NX, x))

    GATHER = ((0, 1), (0, -1), (0, 2), (0, -2), (-2, 1), (2, -1), (-2, 2), (2, -2))

    def part(p, s, chunk, kind):
        cut = 48 if s == 0 else 32
        ref = gathered.at[p, s, (z + chunk + NZ) % NZ]
        if kind == 6:
            return ref.at[pl.ds(0, cut)]
        if kind == 7:
            return ref.at[pl.ds(cut, 80 - cut)]
        return ref

    def gather_out(p, s, kind):
        chunk, by = GATHER[kind]
        ref = part(p, s, chunk, kind)
        return remote(ref, ref, gz_ss.at[p, s, kind], gz_rs.at[p, s, kind], along_z(by))

    def gather_in(p, s, kind):
        chunk, by = GATHER[kind]
        ref = part(p, s, chunk - by, kind)
        return remote(ref, ref, gz_ss.at[p, s, kind], gz_rs.at[p, s, kind], along_z(-by))

    def gather_start(p, absorbed, ropes):
        blank = jnp.zeros((16, 64), F32)
        for s in range(2):
            for k in range(4):
                gathered[p, s, z, k * 16 : (k + 1) * 16, :] = absorbed[
                    s * 16 : (s + 1) * 16, k * 128 : (k + 1) * 128
                ]
            gathered[p, s, z, 64:80, :] = jnp.concatenate([ropes[s], blank], axis=1).astype(BF16)
            for kind in (2, 3):
                send(gather_out(p, s, kind))
        for s in range(2):
            for kind in (0, 1):
                send(gather_out(p, s, kind))

    def gather_mid(p):
        for s in range(2):
            for kind in (2, 3):
                gather_in(p, s, kind).wait_recv()
                send(gather_out(p, s, kind + 2))
                send(gather_out(p, s, kind + 4))

    def gather_end(p, s):
        for kind in (0, 1, 4, 5, 6, 7):
            gather_in(p, s, kind).wait_recv()

    arrive(need_kup)
    absorbed_res = absorb(qn_all[0:32].astype(BF16), kup)
    ropes_res = [qr_all[0:16], qr_all[16:32]]
    gather_start(0, absorbed_res, ropes_res)
    for copy in sib_copies(0):
        send(copy)

    tokens = []
    for i in range(2):
        for n in range(2):
            for k in range(4):
                small[n * 4 + k : n * 4 + k + 1, :] = fresh_all[2 + i, n : n + 1, k * 128 : (k + 1) * 128]
        tokens.append(small[...])
    for i in range(2):
        row = jnp.concatenate([fresh_rope_all[2 + i, 0:1], fresh_rope_all[2 + i, 1:2]], axis=1)
        tokens.append(jnp.broadcast_to(row, (8, 128)))
    pay_b[y] = jnp.concatenate(tokens, axis=0).astype(BF16)
    for k in range(1, NY):
        send(yb_copy((y + k) % NY, y))
    for copy in sib_copies(1):
        send(copy)

    fresh_res = [[fresh_all[s, n : n + 1] for n in range(2)] for s in range(2)]
    fresh_rope_res = [[fresh_rope_all[s, n : n + 1] for n in range(2)] for s in range(2)]
    scores_res = new_scores(scale, absorbed_res, ropes_res, fresh_res, fresh_rope_res)

    def xa_copy(to, frm):
        return remote(xs_a.at[to], xr_a.at[x], xa_ss.at[to], xa_rs.at[frm], (to * NY + y, d))

    def xb_copy(to, frm):
        return remote(xs_b.at[to], xr_b.at[x], xb_ss.at[to], xb_rs.at[frm], (to * NY + y, d))

    def choose_for(to, held, base, width):
        blocks = []
        for r in range(2):
            wanted = dest_x[to * 2 + r]
            block = jnp.zeros((width, 128), F32)
            for j in range(NY):
                for i in range(2):
                    here = ((x * NY + j) * 2 + i).astype(F32)
                    rows = held[j, base + i * width : base + (i + 1) * width, :]
                    block = jnp.where(jnp.broadcast_to(wanted == here, (width, 128)), rows, block)
            blocks.append(block)
        return blocks

    for k in range(1, NY):
        frm = (y + k) % NY
        ya_copy(frm, frm).wait_recv()
    for k in range(1, NX):
        frm = (x + k) % NX
        dx_copy(frm, frm).wait_recv()
    held = pay_a[...].astype(F32)
    for k in (2, 1, 3, 0):
        to = (x + k) % NX
        block = choose_for(to, held, 0, 16) + choose_for(to, held, 32, 8)
        block = jnp.concatenate(block, axis=0).astype(BF16)
        if k:
            xs_a[to] = block
            send(xa_copy(to, x))
        else:
            xr_a[x] = block
    for k in range(1, NY):
        frm = (y + k) % NY
        yb_copy(frm, frm).wait_recv()
    held = pay_b[...].astype(F32)
    for k in (2, 1, 3, 0):
        to = (x + k) % NX
        block = choose_for(to, held, 0, 8) + choose_for(to, held, 16, 8)
        block = jnp.concatenate(block, axis=0).astype(BF16)
        if k:
            xs_b[to] = block
            send(xb_copy(to, x))
        else:
            xr_b[x] = block
    gather_mid(0)
    for k in range(1, NX):
        frm = (x + k) % NX
        xa_copy(frm, frm).wait_recv()
    block = xr_a[0].astype(F32)
    for j in range(1, NX):
        block = block + xr_a[j].astype(F32)
    ropes_inc = [
        jnp.concatenate([block[32 + 8 * r : 40 + 8 * r, 0:64], block[32 + 8 * r : 40 + 8 * r, 64:128]], axis=0)
        for r in range(2)
    ]
    absorbed_inc = absorb(block[0:32].astype(BF16), kup)
    gather_start(1, absorbed_inc, ropes_inc)

    def da_copy(to, frm):
        ref = dest_all.at[pl.ds(g * 2, 2)]
        return remote(ref, ref, da_ss.at[to], da_rs.at[frm], (to, d))

    over_groups(lambda to: da_copy(to, g).start())
    sent_over_groups.append(da_copy)

    for k in range(1, NX):
        frm = (x + k) % NX
        xb_copy(frm, frm).wait_recv()
    block = xr_b[0].astype(F32)
    for j in range(1, NX):
        block = block + xr_b[j].astype(F32)
    fresh_inc, fresh_rope_inc = [], []
    for r in range(2):
        small[...] = block[8 * r : 8 * r + 8]
        fresh_inc.append(
            [
                jnp.concatenate([small[n * 4 + k : n * 4 + k + 1, :] for k in range(4)], axis=1)
                for n in range(2)
            ]
        )
        row = block[16 + 8 * r : 17 + 8 * r]
        fresh_rope_inc.append([row[:, 0:64], row[:, 64:128]])
    scores_inc = new_scores(scale, absorbed_inc, ropes_inc, fresh_inc, fresh_rope_inc)

    def out_copy(p, s, to, frm):
        device = (g, to * 2 + c)
        return remote(zs_bf.at[p, s, to], zr_bf.at[p, s, z], zo_ss.at[p, s, to], zo_rs.at[p, s, frm], device)

    def stat_copy(p, to, frm):
        device = (g, to * 2 + c)
        return remote(zs_st.at[p, to], zr_st.at[p, z], zt_ss.at[p, to], zt_rs.at[p, frm], device)

    FAR_FIRST = (4, 3, 5, 2, 6, 1, 7)

    def partials(p, s, lengths):
        return attend(
            scale, gathered.at[p, s], lat[p, s], rope[p, s], lengths[0, s], z * 512, zs_bf.at[p, s]
        )

    def share(p, s):
        for k in FAR_FIRST:
            send(out_copy(p, s, (z + k) % NZ, z))
        zr_bf[p, s, z] = zs_bf[p, s, z]

    def share_stats(p, fields):
        zs_st[p] = rows_of([fields[0][0], fields[1][0], fields[0][1], fields[1][1]])
        for k in FAR_FIRST:
            send(stat_copy(p, (z + k) % NZ, z))
        zr_st[p, z] = zs_st[p, z]

    def collect(p):
        for k in FAR_FIRST:
            frm = (z + k) % NZ
            for s in range(2):
                out_copy(p, s, frm, frm).wait_recv()
            stat_copy(p, frm, frm).wait_recv()

    arrive(need_res)
    for copy in sib_copies(0):
        copy.wait_recv()
    fields_res = []
    for s in range(2):
        gather_end(0, s)
        fields_res.append(partials(0, s, rlen))
    gather_mid(1)
    arrive(need_inc)
    for copy in sib_copies(1):
        copy.wait_recv()
    fields_inc = []
    for s in range(2):
        gather_end(1, s)
        fields_inc.append(partials(1, s, plen))
        share(1, s)
    share_stats(1, fields_inc)
    arrive(need_vup)
    collect(1)
    for s in range(2):
        share(0, s)
    share_stats(0, fields_res)
    out_inc = finish(zr_bf.at[1], zr_st.at[1], scores_inc, fresh_inc, vup)

    def ret_block(to):
        block = jnp.zeros((16, 128), F32)
        for r in range(2):
            goal = dest_all[g * 2 + r]
            first = (to * 2).astype(F32)
            hit = (goal == first) | (goal == first + 1.0)
            block = jnp.where(jnp.broadcast_to(hit, (16, 128)), out_inc[r * 16 : (r + 1) * 16], block)
        return block.astype(BF16)

    def ret_copy(to, frm):
        return remote(ret_send.at[to], ret_recv.at[g], ret_ss.at[to], ret_rs.at[frm], (to, d))

    def ret_start(to):
        ret_send[to] = ret_block(to)
        ret_copy(to, g).start()

    over_groups(ret_start)
    sent_over_groups.append(ret_copy)
    ret_recv[g] = ret_block(g)

    collect(0)
    out_res = finish(zr_bf.at[0], zr_st.at[0], scores_res, fresh_res, vup)
    out[0:2] = out_res.reshape(2, 2, 8, 128).astype(BF16)

    over_groups(lambda frm: da_copy(frm, frm).wait_recv())
    over_groups(lambda frm: ret_copy(frm, frm).wait_recv())

    def choose(frm, chosen):
        block = ret_recv[frm].astype(F32)
        picked = []
        for i in range(2):
            here = (g * 2 + i).astype(F32)
            hit = (dest_all[frm * 2] == here) | (dest_all[frm * 2 + 1] == here)
            picked.append(jnp.where(jnp.broadcast_to(hit, (16, 128)), block, chosen[i]))
        return tuple(picked)

    zero = jnp.zeros((16, 128), F32)
    chosen = lax.fori_loop(0, NG, choose, (zero, zero))
    for i in range(2):
        out[2 + i] = chosen[i].reshape(2, 8, 128).astype(BF16)

    drain()


def body(
    prompt_latent_cache, prompt_rope, prompt_length, dest_slot, resident_latent, resident_rope,
    resident_length, new_latent, new_rope, query_nope, query_rope, key_up, value_up_weight,
):
    scale = attend_scale(query_nope.shape[-1], query_rope.shape[-1])
    hbm = pl.BlockSpec(memory_space=pltpu.HBM)
    dma = pltpu.SemaphoreType.DMA
    vmem = pltpu.VMEM
    return pl.pallas_call(
        functools.partial(kernel, scale),
        out_shape=jax.ShapeDtypeStruct((4, 2, 8, 128), BF16),
        in_specs=[hbm] * 13,
        out_specs=pl.BlockSpec(memory_space=pltpu.VMEM),
        scratch_shapes=[
            vmem((2, 2, 512, 512), BF16),
            vmem((2, 2, 64, 512), BF16),
            pltpu.SMEM((1, 2), jnp.int32),
            pltpu.SMEM((1, 2), jnp.int32),
            pltpu.SMEM((1, 2), jnp.int32),
            vmem((4, 2, 512), BF16),
            vmem((4, 2, 64), BF16),
            vmem((4, 2, 8, 128), BF16),
            vmem((4, 2, 8, 64), BF16),
            vmem((8, 128, 512), BF16),
            vmem((8, 512, 128), BF16),
            vmem((NX * 2, 1, 128), F32),
            vmem((NG * 2, 1, 128), F32),
            vmem((NY, 48, 128), BF16),
            vmem((NY, 32, 128), BF16),
            vmem((NX, 48, 128), BF16),
            vmem((NX, 32, 128), BF16),
            vmem((NX, 48, 128), BF16),
            vmem((NX, 32, 128), BF16),
            vmem((2, 2, NZ, 80, 128), BF16),
            vmem((2, 2, NZ, 16, 512), BF16),
            vmem((2, NZ, 1, 128), F32),
            vmem((2, 2, NZ, 16, 512), BF16),
            vmem((2, NZ, 1, 128), F32),
            vmem((NG, 16, 128), BF16),
            vmem((NG, 16, 128), BF16),
            vmem((8, 128), F32),
            dma((13,)),
            dma((2, 2)), dma((2, 2)),
            dma((NY,)), dma((NY,)), dma((NY,)), dma((NY,)),
            dma((NX,)), dma((NX,)), dma((NX,)), dma((NX,)),
            dma((NX,)), dma((NX,)),
            dma((NG,)), dma((NG,)),
            dma((2, 2, 8)), dma((2, 2, 8)),
            dma((2, 2, NZ)), dma((2, 2, NZ)),
            dma((2, NZ)), dma((2, NZ)),
            dma((NG,)), dma((NG,)),
        ],
        compiler_params=pltpu.CompilerParams(
            collective_id=0, has_side_effects=True, vmem_limit_bytes=48 << 20
        ),
        name="latent_attend",
    )(*(pltpu.with_memory_space_constraint(a, pltpu.HBM) for a in (
        prompt_latent_cache, prompt_rope, prompt_length, dest_slot, resident_latent, resident_rope,
        resident_length, new_latent, new_rope, query_nope, query_rope, key_up, value_up_weight,
    )))


def solution(mesh):
    placed = (
        P("grp", "dev", None),
        P("grp", None, "dev"),
        P("grp", None),
        P("grp", None),
        P("grp", "dev", None),
        P("grp", None, "dev"),
        P("grp", None),
        P("grp", None, None),
        P("grp", None, None),
        P("grp", None, "dev", None),
        P("grp", None, "dev", None),
        P("dev", None, None),
        P("dev", None, None),
    )
    return jax.shard_map(
        body, mesh=mesh, in_specs=placed, out_specs=P("grp", None, "dev", None), check_vma=False
    )
```

```python
import functools
import math

import jax
import jax.numpy as jnp
from jax import lax
from jax.experimental import pallas as pl
from jax.experimental.pallas import tpu as pltpu
from jax.sharding import PartitionSpec as P

MESH = pl.DeviceIdType.MESH
F32 = jnp.float32
BF16 = jnp.bfloat16
NX, NY, NZ = 4, 8, 8
NG = NX * NY
NEG = -1e30


def attend_scale(nope_width, rotary_width):
    return (0.1 * math.log(40.0) + 1.0) ** 2 / math.sqrt(nope_width + rotary_width)


def iota(shape, axis):
    return lax.broadcasted_iota(jnp.int32, shape, axis)


def columns_of(rows, field):
    n = rows.shape[0]
    hit = iota((n, 16, 128), 2) == iota((n, 16, 128), 1) + 16 * field
    return jnp.sum(jnp.where(hit, jnp.broadcast_to(rows, (n, 16, 128)), 0.0), axis=-1, keepdims=True)


def rows_of(fields):
    n = fields[0].shape[0]
    lane, sub = iota((n, 16, 128), 2), iota((n, 16, 128), 1)
    packed = jnp.zeros((n, 16, 128), F32)
    for f, column in enumerate(fields):
        packed = jnp.where(lane == sub + 16 * f, jnp.broadcast_to(column, (n, 16, 128)), packed)
    return jnp.sum(packed, axis=1, keepdims=True)


def absorb(q32, kup):
    head = iota((32, 512), 0) % 8
    total = jnp.zeros((32, 512), F32)
    for h in range(8):
        total = jnp.where(head == h, jnp.dot(q32, kup[h], preferred_element_type=F32), total)
    return total.astype(BF16)


def new_scores(scale, absorbed, ropes, fresh, fresh_rope):
    step = iota((16, 1), 0) // 8
    out = []
    for s in range(2):
        q = absorbed[s * 16 : (s + 1) * 16].astype(F32)
        pair = []
        for n in range(2):
            v = jnp.sum(q * fresh[s][n], axis=-1, keepdims=True)
            v = v + jnp.sum(ropes[s] * fresh_rope[s][n], axis=-1, keepdims=True)
            v = v * scale
            pair.append(v if n == 0 else jnp.where(step >= 1, v, NEG))
        out.append(pair)
    return out


def attend(scale, gathered, keys, rope, length, offset, out_bf):
    q = jnp.concatenate(
        [gathered[:, k * 16 : (k + 1) * 16, :].reshape(128, 128) for k in range(4)], axis=1
    )
    ropes = gathered[:, 64:80, :].reshape(128, 128)[:, 0:64]
    scores = lax.dot_general(q, keys, (((1,), (1,)), ((), ())), preferred_element_type=F32)
    scores = scale * (scores + jnp.dot(ropes, rope, preferred_element_type=F32))
    live = offset + iota((128, 512), 1) < length
    scores = jnp.where(live, scores, NEG)
    top = jnp.max(scores, axis=-1, keepdims=True)
    weights = jnp.where(live, jnp.exp(scores - top), 0.0)
    total = jnp.sum(weights, axis=-1, keepdims=True)
    summed = jnp.dot(weights.astype(BF16), keys, preferred_element_type=F32)
    summed = summed / jnp.maximum(total, 1.0)
    out_bf[...] = summed.reshape(8, 16, 512).astype(BF16)
    return top.reshape(8, 16, 1), total.reshape(8, 16, 1)


def finish(blocks, stats, fresh_scores, fresh, vup):
    rows = []
    for s in range(2):
        m, l = columns_of(stats[...], s), columns_of(stats[...], 2 + s)
        n0, n1 = fresh_scores[s]
        top = jnp.maximum(jnp.max(m, axis=0), jnp.maximum(n0, n1))
        w = l * jnp.exp(m - top[None])
        w0 = jnp.exp(n0 - top)
        w1 = jnp.where(n1 > NEG, jnp.exp(n1 - top), 0.0)
        under = jnp.sum(w, axis=0) + w0 + w1
        total = w0 * fresh[s][0] + w1 * fresh[s][1]
        for j in range(NZ):
            total = total + w[j] * blocks[s, j].astype(F32)
        rows.append(total / under)
    attended = jnp.concatenate(rows, axis=0).astype(BF16)
    head = iota((32, 128), 0) % 8
    out = jnp.zeros((32, 128), F32)
    for h in range(8):
        out = jnp.where(head == h, jnp.dot(attended, vup[h], preferred_element_type=F32), out)
    return out


def kernel(
    scale,
    plat_hbm, prope_hbm, plen_hbm, dest_hbm, rlat_hbm, rrope_hbm, rlen_hbm, nlat_hbm, nrope_hbm,
    qn_hbm, qr_hbm, kup_hbm, vup_hbm,
    out,
    lat, rope, plen, dest, rlen, nlat, nrope, qn, qr, kup, vup,
    dest_x, dest_all, pay_a, pay_b, xs_a, xs_b, xr_a, xr_b, gathered,
    zs_bf, zs_st, zr_bf, zr_st, ret_send, ret_recv, small,
    load_sem, sib_ss, sib_rs, ya_ss, ya_rs, yb_ss, yb_rs, xa_ss, xa_rs, xb_ss, xb_rs,
    dx_ss, dx_rs, da_ss, da_rs, gz_ss, gz_rs, zo_ss, zo_rs, zt_ss, zt_rs, ret_ss, ret_rs,
):
    g, d = lax.axis_index("grp"), lax.axis_index("dev")
    x, y = g // NY, g % NY
    z, c = d // 2, d % 2

    def along_z(k):
        return (g, ((z + k + NZ) % NZ) * 2 + c)

    def along_y(k):
        return (x * NY + (y + k) % NY, d)

    def along_x(k):
        return (((x + k) % NX) * NY + y, d)

    sibling = (g, z * 2 + 1 - c)

    barrier = pltpu.get_barrier_semaphore()
    peers = [along_y(k) for k in range(1, NY)] + [along_x(k) for k in range(1, NX)]
    peers += [sibling] + [along_z(k) for k in range(1, NZ)]
    for peer in peers:
        pl.semaphore_signal(barrier, inc=1, device_id=peer, device_id_type=MESH)

    half = pl.ds(pl.multiple_of(c * 256, 256), 256)
    loads = [
        pltpu.make_async_copy(src, dst, load_sem.at[i])
        for i, (src, dst) in enumerate(
            [
                (qn_hbm, qn), (qr_hbm, qr), (nlat_hbm, nlat), (nrope_hbm, nrope), (dest_hbm, dest),
                (kup_hbm, kup),
                (rlat_hbm, lat.at[0, :, half, :]), (rrope_hbm, rope.at[0, :, :, half]), (rlen_hbm, rlen),
                (plat_hbm, lat.at[1, :, half, :]), (prope_hbm, rope.at[1, :, :, half]), (plen_hbm, plen),
                (vup_hbm, vup),
            ]
        )
    ]
    need_small, need_kup, need_res, need_inc, need_vup = (
        loads[0:5], loads[5:6], loads[6:9], loads[9:12], loads[12:13]
    )
    for load in loads:
        load.start()
    waiting = list(loads)

    def arrive(wanted):
        for load in wanted:
            load.wait()
            waiting.remove(load)

    sent = []

    def send(copy):
        copy.start()
        sent.append(copy)

    def over_groups(start):
        def step(k, _):
            start((g + k) % NG)
            return 0

        lax.fori_loop(1, NG, step, 0)

    all_sent = []

    def drain():
        for load in waiting:
            load.wait()
        for copy in sent:
            copy.wait_send()
        for copy in all_sent:
            copy.wait_send()

    def remote(src, dst, ss, rs, device):
        return pltpu.make_async_remote_copy(
            src_ref=src, dst_ref=dst, send_sem=ss, recv_sem=rs, device_id=device, device_id_type=MESH
        )

    def sib_copies(p):
        lat_hbm, rope_hbm = ((rlat_hbm, rrope_hbm), (plat_hbm, prope_hbm))[p]
        return (
            remote(lat_hbm, lat.at[p, :, half, :], sib_ss.at[p, 0], sib_rs.at[p, 0], sibling),
            remote(rope_hbm, rope.at[p, :, :, half], sib_ss.at[p, 1], sib_rs.at[p, 1], sibling),
        )

    arrive(need_small)
    qn_all = qn[...].astype(F32).reshape(64, 128)
    qr_all = qr[...].astype(F32).reshape(64, 64)
    fresh_all = nlat[...].astype(F32)
    fresh_rope_all = nrope[...].astype(F32)
    rope_rows = [
        jnp.concatenate([qr_all[s * 16 : s * 16 + 8], qr_all[s * 16 + 8 : s * 16 + 16]], axis=1)
        for s in (2, 3)
    ]
    pay_a[y] = jnp.concatenate([qn_all[32:64]] + rope_rows, axis=0).astype(BF16)
    for i in range(2):
        dest_x[x * 2 + i] = jnp.full((1, 128), dest[0, i].astype(F32))
        dest_all[g * 2 + i] = jnp.full((1, 128), dest[0, i].astype(F32))

    pl.semaphore_wait(barrier, len(peers))

    def ya_copy(to, frm):
        return remote(pay_a.at[y], pay_a.at[y], ya_ss.at[to], ya_rs.at[frm], (x * NY + to, d))

    def yb_copy(to, frm):
        return remote(pay_b.at[y], pay_b.at[y], yb_ss.at[to], yb_rs.at[frm], (x * NY + to, d))

    def dx_copy(to, frm):
        ref = dest_x.at[pl.ds(x * 2, 2)]
        return remote(ref, ref, dx_ss.at[to], dx_rs.at[frm], (to * NY + y, d))

    for k in (4, 3, 5, 2, 6, 1, 7):
        send(ya_copy((y + k) % NY, y))
    for k in range(1, NX):
        send(dx_copy((x + k) % NX, x))

    GATHER = ((0, 1), (0, -1), (0, 2), (0, -2), (-2, 1), (2, -1), (-2, 2), (2, -2))

    def part(p, s, chunk, kind):
        cut = 48 if s == 0 else 32
        ref = gathered.at[p, s, (z + chunk + NZ) % NZ]
        if kind == 6:
            return ref.at[pl.ds(0, cut)]
        if kind == 7:
            return ref.at[pl.ds(cut, 80 - cut)]
        return ref

    def gather_out(p, s, kind):
        chunk, by = GATHER[kind]
        ref = part(p, s, chunk, kind)
        return remote(ref, ref, gz_ss.at[p, s, kind], gz_rs.at[p, s, kind], along_z(by))

    def gather_in(p, s, kind):
        chunk, by = GATHER[kind]
        ref = part(p, s, chunk - by, kind)
        return remote(ref, ref, gz_ss.at[p, s, kind], gz_rs.at[p, s, kind], along_z(-by))

    def gather_start(p, absorbed, ropes):
        blank = jnp.zeros((16, 64), F32)
        for s in range(2):
            for k in range(4):
                gathered[p, s, z, k * 16 : (k + 1) * 16, :] = absorbed[
                    s * 16 : (s + 1) * 16, k * 128 : (k + 1) * 128
                ]
            gathered[p, s, z, 64:80, :] = jnp.concatenate([ropes[s], blank], axis=1).astype(BF16)
            for kind in (2, 3):
                send(gather_out(p, s, kind))
        for s in range(2):
            for kind in (0, 1):
                send(gather_out(p, s, kind))

    def gather_mid(p):
        for s in range(2):
            for kind in (2, 3):
                gather_in(p, s, kind).wait_recv()
                send(gather_out(p, s, kind + 2))
                send(gather_out(p, s, kind + 4))

    def gather_end(p, s):
        for kind in (0, 1, 4, 5, 6, 7):
            gather_in(p, s, kind).wait_recv()

    arrive(need_kup)
    absorbed_res = absorb(qn_all[0:32].astype(BF16), kup)
    ropes_res = [qr_all[0:16], qr_all[16:32]]
    gather_start(0, absorbed_res, ropes_res)
    for copy in sib_copies(0):
        send(copy)

    tokens = []
    for i in range(2):
        for n in range(2):
            for k in range(4):
                small[n * 4 + k : n * 4 + k + 1, :] = fresh_all[2 + i, n : n + 1, k * 128 : (k + 1) * 128]
        tokens.append(small[...])
    for i in range(2):
        row = jnp.concatenate([fresh_rope_all[2 + i, 0:1], fresh_rope_all[2 + i, 1:2]], axis=1)
        tokens.append(jnp.broadcast_to(row, (8, 128)))
    pay_b[y] = jnp.concatenate(tokens, axis=0).astype(BF16)
    for k in range(1, NY):
        send(yb_copy((y + k) % NY, y))
    for copy in sib_copies(1):
        send(copy)

    fresh_res = [[fresh_all[s, n : n + 1] for n in range(2)] for s in range(2)]
    fresh_rope_res = [[fresh_rope_all[s, n : n + 1] for n in range(2)] for s in range(2)]
    scores_res = new_scores(scale, absorbed_res, ropes_res, fresh_res, fresh_rope_res)

    def xa_copy(to, frm):
        return remote(xs_a.at[to], xr_a.at[x], xa_ss.at[to], xa_rs.at[frm], (to * NY + y, d))

    def xb_copy(to, frm):
        return remote(xs_b.at[to], xr_b.at[x], xb_ss.at[to], xb_rs.at[frm], (to * NY + y, d))

    def choose_for(to, held, base, width):
        blocks = []
        for r in range(2):
            wanted = dest_x[to * 2 + r]
            block = jnp.zeros((width, 128), F32)
            for j in range(NY):
                for i in range(2):
                    here = ((x * NY + j) * 2 + i).astype(F32)
                    rows = held[j, base + i * width : base + (i + 1) * width, :]
                    block = jnp.where(jnp.broadcast_to(wanted == here, (width, 128)), rows, block)
            blocks.append(block)
        return blocks

    for k in range(1, NY):
        frm = (y + k) % NY
        ya_copy(frm, frm).wait_recv()
    for k in range(1, NX):
        frm = (x + k) % NX
        dx_copy(frm, frm).wait_recv()
    held = pay_a[...].astype(F32)
    for k in (2, 1, 3, 0):
        to = (x + k) % NX
        block = choose_for(to, held, 0, 16) + choose_for(to, held, 32, 8)
        block = jnp.concatenate(block, axis=0).astype(BF16)
        if k:
            xs_a[to] = block
            send(xa_copy(to, x))
        else:
            xr_a[x] = block
    for k in range(1, NY):
        frm = (y + k) % NY
        yb_copy(frm, frm).wait_recv()
    held = pay_b[...].astype(F32)
    for k in (2, 1, 3, 0):
        to = (x + k) % NX
        block = choose_for(to, held, 0, 8) + choose_for(to, held, 16, 8)
        block = jnp.concatenate(block, axis=0).astype(BF16)
        if k:
            xs_b[to] = block
            send(xb_copy(to, x))
        else:
            xr_b[x] = block
    gather_mid(0)
    for k in range(1, NX):
        frm = (x + k) % NX
        xa_copy(frm, frm).wait_recv()
    block = xr_a[0].astype(F32)
    for j in range(1, NX):
        block = block + xr_a[j].astype(F32)
    ropes_inc = [
        jnp.concatenate([block[32 + 8 * r : 40 + 8 * r, 0:64], block[32 + 8 * r : 40 + 8 * r, 64:128]], axis=0)
        for r in range(2)
    ]
    absorbed_inc = absorb(block[0:32].astype(BF16), kup)
    gather_start(1, absorbed_inc, ropes_inc)

    def da_copy(to):
        ref = dest_all.at[pl.ds(g * 2, 2)]
        return remote(ref, ref, da_ss, da_rs, (to, d))

    over_groups(lambda to: da_copy(to).start())
    da_every = remote(dest_all.at[pl.ds(0, 62)], dest_all.at[pl.ds(0, 62)], da_ss, da_rs, along_y(1))
    all_sent.append(da_every)

    for k in range(1, NX):
        frm = (x + k) % NX
        xb_copy(frm, frm).wait_recv()
    block = xr_b[0].astype(F32)
    for j in range(1, NX):
        block = block + xr_b[j].astype(F32)
    fresh_inc, fresh_rope_inc = [], []
    for r in range(2):
        small[...] = block[8 * r : 8 * r + 8]
        fresh_inc.append(
            [
                jnp.concatenate([small[n * 4 + k : n * 4 + k + 1, :] for k in range(4)], axis=1)
                for n in range(2)
            ]
        )
        row = block[16 + 8 * r : 17 + 8 * r]
        fresh_rope_inc.append([row[:, 0:64], row[:, 64:128]])
    scores_inc = new_scores(scale, absorbed_inc, ropes_inc, fresh_inc, fresh_rope_inc)

    def out_copy(p, s, to, frm):
        device = (g, to * 2 + c)
        return remote(zs_bf.at[p, s, to], zr_bf.at[p, s, z], zo_ss.at[p, s, to], zo_rs.at[p, s, frm], device)

    def stat_copy(p, to, frm):
        device = (g, to * 2 + c)
        return remote(zs_st.at[p, to], zr_st.at[p, z], zt_ss.at[p, to], zt_rs.at[p, frm], device)

    FAR_FIRST = (4, 3, 5, 2, 6, 1, 7)

    def partials(p, s, lengths):
        return attend(
            scale, gathered.at[p, s], lat[p, s], rope[p, s], lengths[0, s], z * 512, zs_bf.at[p, s]
        )

    def share(p, s):
        for k in FAR_FIRST:
            send(out_copy(p, s, (z + k) % NZ, z))
        zr_bf[p, s, z] = zs_bf[p, s, z]

    def share_stats(p, fields):
        zs_st[p] = rows_of([fields[0][0], fields[1][0], fields[0][1], fields[1][1]])
        for k in FAR_FIRST:
            send(stat_copy(p, (z + k) % NZ, z))
        zr_st[p, z] = zs_st[p, z]

    def collect(p):
        for k in FAR_FIRST:
            frm = (z + k) % NZ
            for s in range(2):
                out_copy(p, s, frm, frm).wait_recv()
            stat_copy(p, frm, frm).wait_recv()

    arrive(need_res)
    for copy in sib_copies(0):
        copy.wait_recv()
    fields_res = []
    for s in range(2):
        gather_end(0, s)
        fields_res.append(partials(0, s, rlen))
    gather_mid(1)
    share(0, 0)
    arrive(need_inc)
    for copy in sib_copies(1):
        copy.wait_recv()
    fields_inc = []
    for s in range(2):
        gather_end(1, s)
        fields_inc.append(partials(1, s, plen))
        share(1, s)
    share_stats(1, fields_inc)
    share(0, 1)
    share_stats(0, fields_res)
    arrive(need_vup)
    collect(1)
    out_inc = finish(zr_bf.at[1], zr_st.at[1], scores_inc, fresh_inc, vup)

    def ret_block(to):
        block = jnp.zeros((16, 128), F32)
        for r in range(2):
            goal = dest_all[g * 2 + r]
            first = (to * 2).astype(F32)
            hit = (goal == first) | (goal == first + 1.0)
            block = jnp.where(jnp.broadcast_to(hit, (16, 128)), out_inc[r * 16 : (r + 1) * 16], block)
        return block.astype(BF16)

    def ret_start(to):
        ret_send[to] = ret_block(to)
        remote(ret_send.at[to], ret_recv.at[g], ret_ss, ret_rs, (to, d)).start()

    over_groups(ret_start)
    ret_every = remote(ret_send.at[pl.ds(0, 31)], ret_recv.at[pl.ds(0, 31)], ret_ss, ret_rs, along_y(1))
    all_sent.append(ret_every)
    ret_recv[g] = ret_block(g)

    collect(0)
    out_res = finish(zr_bf.at[0], zr_st.at[0], scores_res, fresh_res, vup)
    out[0:2] = out_res.reshape(2, 2, 8, 128).astype(BF16)

    da_every.wait_recv()
    ret_every.wait_recv()

    def choose(frm, chosen):
        block = ret_recv[frm].astype(F32)
        picked = []
        for i in range(2):
            here = (g * 2 + i).astype(F32)
            hit = (dest_all[frm * 2] == here) | (dest_all[frm * 2 + 1] == here)
            picked.append(jnp.where(jnp.broadcast_to(hit, (16, 128)), block, chosen[i]))
        return tuple(picked)

    zero = jnp.zeros((16, 128), F32)
    chosen = lax.fori_loop(0, NG, choose, (zero, zero))
    for i in range(2):
        out[2 + i] = chosen[i].reshape(2, 8, 128).astype(BF16)

    drain()


def body(
    prompt_latent_cache, prompt_rope, prompt_length, dest_slot, resident_latent, resident_rope,
    resident_length, new_latent, new_rope, query_nope, query_rope, key_up, value_up_weight,
):
    scale = attend_scale(query_nope.shape[-1], query_rope.shape[-1])
    hbm = pl.BlockSpec(memory_space=pltpu.HBM)
    dma = pltpu.SemaphoreType.DMA
    vmem = pltpu.VMEM
    return pl.pallas_call(
        functools.partial(kernel, scale),
        out_shape=jax.ShapeDtypeStruct((4, 2, 8, 128), BF16),
        in_specs=[hbm] * 13,
        out_specs=pl.BlockSpec(memory_space=pltpu.VMEM),
        scratch_shapes=[
            vmem((2, 2, 512, 512), BF16),
            vmem((2, 2, 64, 512), BF16),
            pltpu.SMEM((1, 2), jnp.int32),
            pltpu.SMEM((1, 2), jnp.int32),
            pltpu.SMEM((1, 2), jnp.int32),
            vmem((4, 2, 512), BF16),
            vmem((4, 2, 64), BF16),
            vmem((4, 2, 8, 128), BF16),
            vmem((4, 2, 8, 64), BF16),
            vmem((8, 128, 512), BF16),
            vmem((8, 512, 128), BF16),
            vmem((NX * 2, 1, 128), F32),
            vmem((NG * 2, 1, 128), F32),
            vmem((NY, 48, 128), BF16),
            vmem((NY, 32, 128), BF16),
            vmem((NX, 48, 128), BF16),
            vmem((NX, 32, 128), BF16),
            vmem((NX, 48, 128), BF16),
            vmem((NX, 32, 128), BF16),
            vmem((2, 2, NZ, 80, 128), BF16),
            vmem((2, 2, NZ, 16, 512), BF16),
            vmem((2, NZ, 1, 128), F32),
            vmem((2, 2, NZ, 16, 512), BF16),
            vmem((2, NZ, 1, 128), F32),
            vmem((NG, 16, 128), BF16),
            vmem((NG, 16, 128), BF16),
            vmem((8, 128), F32),
            dma((13,)),
            dma((2, 2)), dma((2, 2)),
            dma((NY,)), dma((NY,)), dma((NY,)), dma((NY,)),
            dma((NX,)), dma((NX,)), dma((NX,)), dma((NX,)),
            dma((NX,)), dma((NX,)),
            dma, dma,
            dma((2, 2, 8)), dma((2, 2, 8)),
            dma((2, 2, NZ)), dma((2, 2, NZ)),
            dma((2, NZ)), dma((2, NZ)),
            dma, dma,
        ],
        compiler_params=pltpu.CompilerParams(
            collective_id=0, has_side_effects=True, vmem_limit_bytes=48 << 20
        ),
        name="latent_attend",
    )(*(pltpu.with_memory_space_constraint(a, pltpu.HBM) for a in (
        prompt_latent_cache, prompt_rope, prompt_length, dest_slot, resident_latent, resident_rope,
        resident_length, new_latent, new_rope, query_nope, query_rope, key_up, value_up_weight,
    )))


def solution(mesh):
    placed = (
        P("grp", "dev", None),
        P("grp", None, "dev"),
        P("grp", None),
        P("grp", None),
        P("grp", "dev", None),
        P("grp", None, "dev"),
        P("grp", None),
        P("grp", None, None),
        P("grp", None, None),
        P("grp", None, "dev", None),
        P("grp", None, "dev", None),
        P("dev", None, None),
        P("dev", None, None),
    )
    return jax.shard_map(
        body, mesh=mesh, in_specs=placed, out_specs=P("grp", None, "dev", None), check_vma=False
    )
```

```python
import functools
import math

import jax
import jax.numpy as jnp
from jax import lax
from jax.experimental import pallas as pl
from jax.experimental.pallas import tpu as pltpu
from jax.sharding import PartitionSpec as P

MESH = pl.DeviceIdType.MESH
F32 = jnp.float32
BF16 = jnp.bfloat16
NX, NY, NZ = 4, 8, 8
NG = NX * NY
NEG = -1e30


def attend_scale(nope_width, rotary_width):
    return (0.1 * math.log(40.0) + 1.0) ** 2 / math.sqrt(nope_width + rotary_width)


def iota(shape, axis):
    return lax.broadcasted_iota(jnp.int32, shape, axis)


def columns_of(rows, field):
    n = rows.shape[0]
    hit = iota((n, 16, 128), 2) == iota((n, 16, 128), 1) + 16 * field
    return jnp.sum(jnp.where(hit, jnp.broadcast_to(rows, (n, 16, 128)), 0.0), axis=-1, keepdims=True)


def rows_of(fields):
    n = fields[0].shape[0]
    lane, sub = iota((n, 16, 128), 2), iota((n, 16, 128), 1)
    packed = jnp.zeros((n, 16, 128), F32)
    for f, column in enumerate(fields):
        packed = jnp.where(lane == sub + 16 * f, jnp.broadcast_to(column, (n, 16, 128)), packed)
    return jnp.sum(packed, axis=1, keepdims=True)


def absorb(q32, kup):
    head = iota((32, 512), 0) % 8
    total = jnp.zeros((32, 512), F32)
    for h in range(8):
        total = jnp.where(head == h, jnp.dot(q32, kup[h], preferred_element_type=F32), total)
    return total.astype(BF16)


def new_scores(scale, absorbed, ropes, fresh, fresh_rope):
    step = iota((16, 1), 0) // 8
    out = []
    for s in range(2):
        q = absorbed[s * 16 : (s + 1) * 16].astype(F32)
        pair = []
        for n in range(2):
            v = jnp.sum(q * fresh[s][n], axis=-1, keepdims=True)
            v = v + jnp.sum(ropes[s] * fresh_rope[s][n], axis=-1, keepdims=True)
            v = v * scale
            pair.append(v if n == 0 else jnp.where(step >= 1, v, NEG))
        out.append(pair)
    return out


def attend(scale, gathered, chunks, keys, rope, length, offset, out_bf):
    n = len(chunks)
    rows = [gathered[chunk] for chunk in chunks]
    q = jnp.concatenate(
        [jnp.concatenate([r[k * 16 : (k + 1) * 16] for r in rows], axis=0) for k in range(4)], axis=1
    )
    ropes = jnp.concatenate([r[64:80] for r in rows], axis=0)[:, 0:64]
    scores = lax.dot_general(q, keys, (((1,), (1,)), ((), ())), preferred_element_type=F32)
    scores = scale * (scores + jnp.dot(ropes, rope, preferred_element_type=F32))
    live = offset + iota((n * 16, 512), 1) < length
    scores = jnp.where(live, scores, NEG)
    top = jnp.max(scores, axis=-1, keepdims=True)
    weights = jnp.where(live, jnp.exp(scores - top), 0.0)
    total = jnp.sum(weights, axis=-1, keepdims=True)
    summed = jnp.dot(weights.astype(BF16), keys, preferred_element_type=F32)
    summed = (summed / jnp.maximum(total, 1.0)).astype(BF16)
    for i, chunk in enumerate(chunks):
        out_bf[chunk] = summed[i * 16 : (i + 1) * 16]
    return top.reshape(n, 16, 1), total.reshape(n, 16, 1)


def finish(blocks, stats, fresh_scores, fresh, vup):
    rows = []
    for s in range(2):
        m, l = columns_of(stats[...], s), columns_of(stats[...], 2 + s)
        n0, n1 = fresh_scores[s]
        top = jnp.maximum(jnp.max(m, axis=0), jnp.maximum(n0, n1))
        w = l * jnp.exp(m - top[None])
        w0 = jnp.exp(n0 - top)
        w1 = jnp.where(n1 > NEG, jnp.exp(n1 - top), 0.0)
        under = jnp.sum(w, axis=0) + w0 + w1
        total = w0 * fresh[s][0] + w1 * fresh[s][1]
        for j in range(NZ):
            total = total + w[j] * blocks[s, j].astype(F32)
        rows.append(total / under)
    attended = jnp.concatenate(rows, axis=0).astype(BF16)
    head = iota((32, 128), 0) % 8
    out = jnp.zeros((32, 128), F32)
    for h in range(8):
        out = jnp.where(head == h, jnp.dot(attended, vup[h], preferred_element_type=F32), out)
    return out


def kernel(
    scale,
    plat_hbm, prope_hbm, plen_hbm, dest_hbm, rlat_hbm, rrope_hbm, rlen_hbm, nlat_hbm, nrope_hbm,
    qn_hbm, qr_hbm, kup_hbm, vup_hbm,
    out,
    lat, rope, plen, dest, rlen, nlat, nrope, qn, qr, kup, vup,
    dest_x, dest_all, pay_a, pay_b, xs_a, xs_b, xr_a, xr_b, gathered,
    zs_bf, zs_st, zr_bf, zr_st, ret_send, ret_recv, small,
    load_sem, sib_ss, sib_rs, ya_ss, ya_rs, yb_ss, yb_rs, xa_ss, xa_rs, xb_ss, xb_rs,
    dx_ss, dx_rs, da_ss, da_rs, gz_ss, gz_rs, zo_ss, zo_rs, zt_ss, zt_rs, ret_ss, ret_rs,
):
    g, d = lax.axis_index("grp"), lax.axis_index("dev")
    x, y = g // NY, g % NY
    z, c = d // 2, d % 2

    def along_z(k):
        return (g, ((z + k + NZ) % NZ) * 2 + c)

    def along_y(k):
        return (x * NY + (y + k) % NY, d)

    def along_x(k):
        return (((x + k) % NX) * NY + y, d)

    sibling = (g, z * 2 + 1 - c)

    barrier = pltpu.get_barrier_semaphore()
    peers = [along_y(k) for k in range(1, NY)] + [along_x(k) for k in range(1, NX)]
    peers += [sibling] + [along_z(k) for k in range(1, NZ)]
    for peer in peers:
        pl.semaphore_signal(barrier, inc=1, device_id=peer, device_id_type=MESH)

    half = pl.ds(pl.multiple_of(c * 256, 256), 256)
    loads = [
        pltpu.make_async_copy(src, dst, load_sem.at[i])
        for i, (src, dst) in enumerate(
            [
                (qn_hbm, qn), (qr_hbm, qr), (nlat_hbm, nlat), (nrope_hbm, nrope), (dest_hbm, dest),
                (kup_hbm, kup),
                (rlat_hbm, lat.at[0, :, half, :]), (rrope_hbm, rope.at[0, :, :, half]), (rlen_hbm, rlen),
                (plat_hbm, lat.at[1, :, half, :]), (prope_hbm, rope.at[1, :, :, half]), (plen_hbm, plen),
                (vup_hbm, vup),
            ]
        )
    ]
    need_small, need_kup, need_res, need_inc, need_vup = (
        loads[0:5], loads[5:6], loads[6:9], loads[9:12], loads[12:13]
    )
    for load in loads:
        load.start()
    waiting = list(loads)

    def arrive(wanted):
        for load in wanted:
            load.wait()
            waiting.remove(load)

    sent = []

    def send(copy):
        copy.start()
        sent.append(copy)

    def over_groups(start):
        def step(k, _):
            start((g + k) % NG)
            return 0

        lax.fori_loop(1, NG, step, 0)

    all_sent = []

    def drain():
        for load in waiting:
            load.wait()
        for copy in sent:
            copy.wait_send()
        for copy in all_sent:
            copy.wait_send()

    def remote(src, dst, ss, rs, device):
        return pltpu.make_async_remote_copy(
            src_ref=src, dst_ref=dst, send_sem=ss, recv_sem=rs, device_id=device, device_id_type=MESH
        )

    def sib_copies(p):
        lat_hbm, rope_hbm = ((rlat_hbm, rrope_hbm), (plat_hbm, prope_hbm))[p]
        return (
            remote(lat_hbm, lat.at[p, :, half, :], sib_ss.at[p, 0], sib_rs.at[p, 0], sibling),
            remote(rope_hbm, rope.at[p, :, :, half], sib_ss.at[p, 1], sib_rs.at[p, 1], sibling),
        )

    arrive(need_small)
    qn_all = qn[...].astype(F32).reshape(64, 128)
    qr_all = qr[...].astype(F32).reshape(64, 64)
    fresh_all = nlat[...].astype(F32)
    fresh_rope_all = nrope[...].astype(F32)
    rope_rows = [
        jnp.concatenate([qr_all[s * 16 : s * 16 + 8], qr_all[s * 16 + 8 : s * 16 + 16]], axis=1)
        for s in (2, 3)
    ]
    pay_a[y] = jnp.concatenate([qn_all[32:64]] + rope_rows, axis=0).astype(BF16)
    for i in range(2):
        dest_x[x * 2 + i] = jnp.full((1, 128), dest[0, i].astype(F32))
        dest_all[g * 2 + i] = jnp.full((1, 128), dest[0, i].astype(F32))

    pl.semaphore_wait(barrier, len(peers))

    def ya_copy(to, frm):
        return remote(pay_a.at[y], pay_a.at[y], ya_ss.at[to], ya_rs.at[frm], (x * NY + to, d))

    def yb_copy(to, frm):
        return remote(pay_b.at[y], pay_b.at[y], yb_ss.at[to], yb_rs.at[frm], (x * NY + to, d))

    def dx_copy(to, frm):
        ref = dest_x.at[pl.ds(x * 2, 2)]
        return remote(ref, ref, dx_ss.at[to], dx_rs.at[frm], (to * NY + y, d))

    for k in (4, 3, 5, 2, 6, 1, 7):
        send(ya_copy((y + k) % NY, y))
    for k in range(1, NX):
        send(dx_copy((x + k) % NX, x))

    GATHER = ((0, 1), (0, -1), (0, 2), (0, -2), (-2, 1), (2, -1), (-2, 2), (2, -2))

    def part(p, s, chunk, kind):
        cut = 48 if s == 0 else 32
        ref = gathered.at[p, s, (z + chunk + NZ) % NZ]
        if kind == 6:
            return ref.at[pl.ds(0, cut)]
        if kind == 7:
            return ref.at[pl.ds(cut, 80 - cut)]
        return ref

    def gather_out(p, s, kind):
        chunk, by = GATHER[kind]
        ref = part(p, s, chunk, kind)
        return remote(ref, ref, gz_ss.at[p, s, kind], gz_rs.at[p, s, kind], along_z(by))

    def gather_in(p, s, kind):
        chunk, by = GATHER[kind]
        ref = part(p, s, chunk - by, kind)
        return remote(ref, ref, gz_ss.at[p, s, kind], gz_rs.at[p, s, kind], along_z(-by))

    def gather_start(p, absorbed, ropes):
        blank = jnp.zeros((16, 64), F32)
        for s in range(2):
            for k in range(4):
                gathered[p, s, z, k * 16 : (k + 1) * 16, :] = absorbed[
                    s * 16 : (s + 1) * 16, k * 128 : (k + 1) * 128
                ]
            gathered[p, s, z, 64:80, :] = jnp.concatenate([ropes[s], blank], axis=1).astype(BF16)
            for kind in (2, 3):
                send(gather_out(p, s, kind))
        for s in range(2):
            for kind in (0, 1):
                send(gather_out(p, s, kind))

    def gather_mid(p):
        for s in range(2):
            for kind in (2, 3):
                gather_in(p, s, kind).wait_recv()
                send(gather_out(p, s, kind + 2))
                send(gather_out(p, s, kind + 4))

    def gather_end(p, s):
        for kind in (0, 1, 4, 5, 6, 7):
            gather_in(p, s, kind).wait_recv()

    arrive(need_kup)
    absorbed_res = absorb(qn_all[0:32].astype(BF16), kup)
    ropes_res = [qr_all[0:16], qr_all[16:32]]
    gather_start(0, absorbed_res, ropes_res)
    for copy in sib_copies(0):
        send(copy)

    tokens = []
    for i in range(2):
        for n in range(2):
            for k in range(4):
                small[n * 4 + k : n * 4 + k + 1, :] = fresh_all[2 + i, n : n + 1, k * 128 : (k + 1) * 128]
        tokens.append(small[...])
    for i in range(2):
        row = jnp.concatenate([fresh_rope_all[2 + i, 0:1], fresh_rope_all[2 + i, 1:2]], axis=1)
        tokens.append(jnp.broadcast_to(row, (8, 128)))
    pay_b[y] = jnp.concatenate(tokens, axis=0).astype(BF16)
    for k in range(1, NY):
        send(yb_copy((y + k) % NY, y))
    for copy in sib_copies(1):
        send(copy)

    fresh_res = [[fresh_all[s, n : n + 1] for n in range(2)] for s in range(2)]
    fresh_rope_res = [[fresh_rope_all[s, n : n + 1] for n in range(2)] for s in range(2)]
    scores_res = new_scores(scale, absorbed_res, ropes_res, fresh_res, fresh_rope_res)

    def xa_copy(to, frm):
        return remote(xs_a.at[to], xr_a.at[x], xa_ss.at[to], xa_rs.at[frm], (to * NY + y, d))

    def xb_copy(to, frm):
        return remote(xs_b.at[to], xr_b.at[x], xb_ss.at[to], xb_rs.at[frm], (to * NY + y, d))

    def choose_for(to, held, base, width):
        blocks = []
        for r in range(2):
            wanted = dest_x[to * 2 + r]
            block = jnp.zeros((width, 128), F32)
            for j in range(NY):
                for i in range(2):
                    here = ((x * NY + j) * 2 + i).astype(F32)
                    rows = held[j, base + i * width : base + (i + 1) * width, :]
                    block = jnp.where(jnp.broadcast_to(wanted == here, (width, 128)), rows, block)
            blocks.append(block)
        return blocks

    for k in range(1, NY):
        frm = (y + k) % NY
        ya_copy(frm, frm).wait_recv()
    for k in range(1, NX):
        frm = (x + k) % NX
        dx_copy(frm, frm).wait_recv()
    held = pay_a[...].astype(F32)
    for k in (2, 1, 3, 0):
        to = (x + k) % NX
        block = choose_for(to, held, 0, 16) + choose_for(to, held, 32, 8)
        block = jnp.concatenate(block, axis=0).astype(BF16)
        if k:
            xs_a[to] = block
            send(xa_copy(to, x))
        else:
            xr_a[x] = block
    gather_mid(0)
    for k in range(1, NX):
        frm = (x + k) % NX
        xa_copy(frm, frm).wait_recv()
    block = xr_a[0].astype(F32)
    for j in range(1, NX):
        block = block + xr_a[j].astype(F32)
    ropes_inc = [
        jnp.concatenate([block[32 + 8 * r : 40 + 8 * r, 0:64], block[32 + 8 * r : 40 + 8 * r, 64:128]], axis=0)
        for r in range(2)
    ]
    absorbed_inc = absorb(block[0:32].astype(BF16), kup)
    gather_start(1, absorbed_inc, ropes_inc)

    def out_copy(p, s, to, frm):
        device = (g, to * 2 + c)
        return remote(zs_bf.at[p, s, to], zr_bf.at[p, s, z], zo_ss.at[p, s, to], zo_rs.at[p, s, frm], device)

    def stat_copy(p, to, frm):
        device = (g, to * 2 + c)
        return remote(zs_st.at[p, to], zr_st.at[p, z], zt_ss.at[p, to], zt_rs.at[p, frm], device)

    FAR_FIRST = (4, 3, 5, 2, 6, 1, 7)

    NEAR, REST = (0, 2, 6, 1, 7), (4, 3, 5)

    def partials(p, s, lengths, offsets):
        chunks = [(z + k) % NZ for k in offsets]
        return attend(
            scale, gathered.at[p, s], chunks, lat[p, s], rope[p, s], lengths[0, s], z * 512, zs_bf.at[p, s]
        )

    def share(p, s, offsets):
        for k in offsets:
            if k:
                send(out_copy(p, s, (z + k) % NZ, z))
            else:
                zr_bf[p, s, z] = zs_bf[p, s, z]

    def share_stats(p, offsets, fields):
        rows = rows_of([fields[0][0], fields[1][0], fields[0][1], fields[1][1]])
        for i, k in enumerate(offsets):
            to = (z + k) % NZ
            if k:
                zs_st[p, to] = rows[i]
                send(stat_copy(p, to, z))
            else:
                zr_st[p, z] = rows[i]

    def collect(p):
        for k in FAR_FIRST:
            frm = (z + k) % NZ
            for s in range(2):
                out_copy(p, s, frm, frm).wait_recv()
            stat_copy(p, frm, frm).wait_recv()

    arrive(need_res)
    for copy in sib_copies(0):
        copy.wait_recv()
    fields_res = []
    for s in range(2):
        gather_end(0, s)
        fields_res.append(partials(0, s, rlen, NEAR + REST))
    for k in range(1, NY):
        frm = (y + k) % NY
        yb_copy(frm, frm).wait_recv()
    held = pay_b[...].astype(F32)
    for k in (2, 1, 3, 0):
        to = (x + k) % NX
        block = choose_for(to, held, 0, 8) + choose_for(to, held, 16, 8)
        block = jnp.concatenate(block, axis=0).astype(BF16)
        if k:
            xs_b[to] = block
            send(xb_copy(to, x))
        else:
            xr_b[x] = block
    gather_mid(1)
    def da_copy(to):
        ref = dest_all.at[pl.ds(g * 2, 2)]
        return remote(ref, ref, da_ss, da_rs, (to, d))

    over_groups(lambda to: da_copy(to).start())
    da_every = remote(dest_all.at[pl.ds(0, 62)], dest_all.at[pl.ds(0, 62)], da_ss, da_rs, along_y(1))
    all_sent.append(da_every)

    arrive(need_inc)
    for copy in sib_copies(1):
        copy.wait_recv()
    for offsets, kinds in ((NEAR, (0, 1)), (REST, (4, 5, 6, 7))):
        fields_inc = []
        for s in range(2):
            for kind in kinds:
                gather_in(1, s, kind).wait_recv()
            fields_inc.append(partials(1, s, plen, offsets))
            share(1, s, offsets)
        share_stats(1, offsets, fields_inc)
    share(0, 0, REST + NEAR)
    share(0, 1, REST + NEAR)
    share_stats(0, NEAR + REST, fields_res)
    for k in range(1, NX):
        frm = (x + k) % NX
        xb_copy(frm, frm).wait_recv()
    block = xr_b[0].astype(F32)
    for j in range(1, NX):
        block = block + xr_b[j].astype(F32)
    fresh_inc, fresh_rope_inc = [], []
    for r in range(2):
        small[...] = block[8 * r : 8 * r + 8]
        fresh_inc.append(
            [
                jnp.concatenate([small[n * 4 + k : n * 4 + k + 1, :] for k in range(4)], axis=1)
                for n in range(2)
            ]
        )
        row = block[16 + 8 * r : 17 + 8 * r]
        fresh_rope_inc.append([row[:, 0:64], row[:, 64:128]])
    scores_inc = new_scores(scale, absorbed_inc, ropes_inc, fresh_inc, fresh_rope_inc)

    arrive(need_vup)
    collect(1)
    out_inc = finish(zr_bf.at[1], zr_st.at[1], scores_inc, fresh_inc, vup)

    def ret_block(to):
        block = jnp.zeros((16, 128), F32)
        for r in range(2):
            goal = dest_all[g * 2 + r]
            first = (to * 2).astype(F32)
            hit = (goal == first) | (goal == first + 1.0)
            block = jnp.where(jnp.broadcast_to(hit, (16, 128)), out_inc[r * 16 : (r + 1) * 16], block)
        return block.astype(BF16)

    def ret_start(to):
        ret_send[to] = ret_block(to)
        remote(ret_send.at[to], ret_recv.at[g], ret_ss, ret_rs, (to, d)).start()

    for ky in FAR_FIRST + (0,):
        for kx in (2, 1, 3, 0):
            if kx or ky:
                ret_start(((x + kx) % NX) * NY + (y + ky) % NY)
    ret_every = remote(ret_send.at[pl.ds(0, 31)], ret_recv.at[pl.ds(0, 31)], ret_ss, ret_rs, along_y(1))
    all_sent.append(ret_every)
    ret_recv[g] = ret_block(g)

    collect(0)
    out_res = finish(zr_bf.at[0], zr_st.at[0], scores_res, fresh_res, vup)
    out[0:2] = out_res.reshape(2, 2, 8, 128).astype(BF16)

    da_every.wait_recv()
    ret_every.wait_recv()

    def choose(frm, chosen):
        block = ret_recv[frm].astype(F32)
        picked = []
        for i in range(2):
            here = (g * 2 + i).astype(F32)
            hit = (dest_all[frm * 2] == here) | (dest_all[frm * 2 + 1] == here)
            picked.append(jnp.where(jnp.broadcast_to(hit, (16, 128)), block, chosen[i]))
        return tuple(picked)

    zero = jnp.zeros((16, 128), F32)
    chosen = lax.fori_loop(0, NG, choose, (zero, zero))
    for i in range(2):
        out[2 + i] = chosen[i].reshape(2, 8, 128).astype(BF16)

    drain()


def body(
    prompt_latent_cache, prompt_rope, prompt_length, dest_slot, resident_latent, resident_rope,
    resident_length, new_latent, new_rope, query_nope, query_rope, key_up, value_up_weight,
):
    scale = attend_scale(query_nope.shape[-1], query_rope.shape[-1])
    hbm = pl.BlockSpec(memory_space=pltpu.HBM)
    dma = pltpu.SemaphoreType.DMA
    vmem = pltpu.VMEM
    return pl.pallas_call(
        functools.partial(kernel, scale),
        out_shape=jax.ShapeDtypeStruct((4, 2, 8, 128), BF16),
        in_specs=[hbm] * 13,
        out_specs=pl.BlockSpec(memory_space=pltpu.VMEM),
        scratch_shapes=[
            vmem((2, 2, 512, 512), BF16),
            vmem((2, 2, 64, 512), BF16),
            pltpu.SMEM((1, 2), jnp.int32),
            pltpu.SMEM((1, 2), jnp.int32),
            pltpu.SMEM((1, 2), jnp.int32),
            vmem((4, 2, 512), BF16),
            vmem((4, 2, 64), BF16),
            vmem((4, 2, 8, 128), BF16),
            vmem((4, 2, 8, 64), BF16),
            vmem((8, 128, 512), BF16),
            vmem((8, 512, 128), BF16),
            vmem((NX * 2, 1, 128), F32),
            vmem((NG * 2, 1, 128), F32),
            vmem((NY, 48, 128), BF16),
            vmem((NY, 32, 128), BF16),
            vmem((NX, 48, 128), BF16),
            vmem((NX, 32, 128), BF16),
            vmem((NX, 48, 128), BF16),
            vmem((NX, 32, 128), BF16),
            vmem((2, 2, NZ, 80, 128), BF16),
            vmem((2, 2, NZ, 16, 512), BF16),
            vmem((2, NZ, 1, 128), F32),
            vmem((2, 2, NZ, 16, 512), BF16),
            vmem((2, NZ, 1, 128), F32),
            vmem((NG, 16, 128), BF16),
            vmem((NG, 16, 128), BF16),
            vmem((8, 128), F32),
            dma((13,)),
            dma((2, 2)), dma((2, 2)),
            dma((NY,)), dma((NY,)), dma((NY,)), dma((NY,)),
            dma((NX,)), dma((NX,)), dma((NX,)), dma((NX,)),
            dma((NX,)), dma((NX,)),
            dma, dma,
            dma((2, 2, 8)), dma((2, 2, 8)),
            dma((2, 2, NZ)), dma((2, 2, NZ)),
            dma((2, NZ)), dma((2, NZ)),
            dma, dma,
        ],
        compiler_params=pltpu.CompilerParams(
            collective_id=0, has_side_effects=True, vmem_limit_bytes=48 << 20
        ),
        name="latent_attend",
    )(*(pltpu.with_memory_space_constraint(a, pltpu.HBM) for a in (
        prompt_latent_cache, prompt_rope, prompt_length, dest_slot, resident_latent, resident_rope,
        resident_length, new_latent, new_rope, query_nope, query_rope, key_up, value_up_weight,
    )))


def solution(mesh):
    placed = (
        P("grp", "dev", None),
        P("grp", None, "dev"),
        P("grp", None),
        P("grp", None),
        P("grp", "dev", None),
        P("grp", None, "dev"),
        P("grp", None),
        P("grp", None, None),
        P("grp", None, None),
        P("grp", None, "dev", None),
        P("grp", None, "dev", None),
        P("dev", None, None),
        P("dev", None, None),
    )
    return jax.shard_map(
        body, mesh=mesh, in_specs=placed, out_specs=P("grp", None, "dev", None), check_vma=False
    )
```

```python
import functools
import math

import jax
import jax.numpy as jnp
from jax import lax
from jax.experimental import pallas as pl
from jax.experimental.pallas import tpu as pltpu
from jax.sharding import PartitionSpec as P

MESH = pl.DeviceIdType.MESH
F32 = jnp.float32
BF16 = jnp.bfloat16
NX, NY, NZ = 4, 8, 8
NG = NX * NY
NEG = -1e30


def attend_scale(nope_width, rotary_width):
    return (0.1 * math.log(40.0) + 1.0) ** 2 / math.sqrt(nope_width + rotary_width)


def iota(shape, axis):
    return lax.broadcasted_iota(jnp.int32, shape, axis)


def columns_of(rows, field):
    n = rows.shape[0]
    hit = iota((n, 16, 128), 2) == iota((n, 16, 128), 1) + 16 * field
    return jnp.sum(jnp.where(hit, jnp.broadcast_to(rows, (n, 16, 128)), 0.0), axis=-1, keepdims=True)


def rows_of(fields):
    n = fields[0].shape[0]
    lane, sub = iota((n, 16, 128), 2), iota((n, 16, 128), 1)
    packed = jnp.zeros((n, 16, 128), F32)
    for f, column in enumerate(fields):
        packed = jnp.where(lane == sub + 16 * f, jnp.broadcast_to(column, (n, 16, 128)), packed)
    return jnp.sum(packed, axis=1, keepdims=True)


def absorb(q32, kup):
    head = iota((32, 512), 0) % 8
    total = jnp.zeros((32, 512), F32)
    for h in range(8):
        total = jnp.where(head == h, jnp.dot(q32, kup[h], preferred_element_type=F32), total)
    return total.astype(BF16)


def new_scores(scale, absorbed, ropes, fresh, fresh_rope):
    step = iota((16, 1), 0) // 8
    out = []
    for s in range(2):
        q = absorbed[s * 16 : (s + 1) * 16].astype(F32)
        pair = []
        for n in range(2):
            v = jnp.sum(q * fresh[s][n], axis=-1, keepdims=True)
            v = v + jnp.sum(ropes[s] * fresh_rope[s][n], axis=-1, keepdims=True)
            v = v * scale
            pair.append(v if n == 0 else jnp.where(step >= 1, v, NEG))
        out.append(pair)
    return out


def attend(scale, gathered, chunks, keys, rope, length, offset, out_bf):
    n = len(chunks)
    rows = [gathered[chunk] for chunk in chunks]
    q = jnp.concatenate(
        [jnp.concatenate([r[k * 16 : (k + 1) * 16] for r in rows], axis=0) for k in range(4)], axis=1
    )
    ropes = jnp.concatenate([r[64:80] for r in rows], axis=0)[:, 0:64]
    scores = lax.dot_general(q, keys, (((1,), (1,)), ((), ())), preferred_element_type=F32)
    scores = scale * (scores + jnp.dot(ropes, rope, preferred_element_type=F32))
    live = offset + iota((n * 16, 512), 1) < length
    scores = jnp.where(live, scores, NEG)
    top = jnp.max(scores, axis=-1, keepdims=True)
    weights = jnp.where(live, jnp.exp(scores - top), 0.0)
    total = jnp.sum(weights, axis=-1, keepdims=True)
    summed = jnp.dot(weights.astype(BF16), keys, preferred_element_type=F32)
    summed = (summed / jnp.maximum(total, 1.0)).astype(BF16)
    for i, chunk in enumerate(chunks):
        out_bf[chunk] = summed[i * 16 : (i + 1) * 16]
    return top.reshape(n, 16, 1), total.reshape(n, 16, 1)


def finish(blocks, stats, fresh_scores, fresh, vup):
    rows = []
    for s in range(2):
        m, l = columns_of(stats[...], s), columns_of(stats[...], 2 + s)
        n0, n1 = fresh_scores[s]
        top = jnp.maximum(jnp.max(m, axis=0), jnp.maximum(n0, n1))
        w = l * jnp.exp(m - top[None])
        w0 = jnp.exp(n0 - top)
        w1 = jnp.where(n1 > NEG, jnp.exp(n1 - top), 0.0)
        under = jnp.sum(w, axis=0) + w0 + w1
        total = w0 * fresh[s][0] + w1 * fresh[s][1]
        for j in range(NZ):
            total = total + w[j] * blocks[s, j].astype(F32)
        rows.append(total / under)
    attended = jnp.concatenate(rows, axis=0).astype(BF16)
    head = iota((32, 128), 0) % 8
    out = jnp.zeros((32, 128), F32)
    for h in range(8):
        out = jnp.where(head == h, jnp.dot(attended, vup[h], preferred_element_type=F32), out)
    return out


def kernel(
    scale,
    plat_hbm, prope_hbm, plen_hbm, dest_hbm, rlat_hbm, rrope_hbm, rlen_hbm, nlat_hbm, nrope_hbm,
    qn_hbm, qr_hbm, kup_hbm, vup_hbm,
    out,
    lat, rope, plen, dest, rlen, nlat, nrope, qn, qr, kup, vup,
    dest_x, dest_all, pay_a, pay_b, xs_a, xs_b, xr_a, xr_b, gathered,
    zs_bf, zs_st, zr_bf, zr_st, ret_send, ret_recv, small,
    load_sem, sib_ss, sib_rs, ya_ss, ya_rs, yb_ss, yb_rs, xa_ss, xa_rs, xb_ss, xb_rs,
    dx_ss, dx_rs, da_ss, da_rs, gz_ss, gz_rs, zo_ss, zo_rs, zt_ss, zt_rs, ret_ss, ret_rs,
):
    g, d = lax.axis_index("grp"), lax.axis_index("dev")
    x, y = g // NY, g % NY
    z, c = d // 2, d % 2

    def along_z(k):
        return (g, ((z + k + NZ) % NZ) * 2 + c)

    def along_y(k):
        return (x * NY + (y + k) % NY, d)

    def along_x(k):
        return (((x + k) % NX) * NY + y, d)

    sibling = (g, z * 2 + 1 - c)

    barrier = pltpu.get_barrier_semaphore()
    peers = [along_y(k) for k in range(1, NY)] + [along_x(k) for k in range(1, NX)]
    peers += [sibling] + [along_z(k) for k in range(1, NZ)]
    for peer in peers:
        pl.semaphore_signal(barrier, inc=1, device_id=peer, device_id_type=MESH)

    half = pl.ds(pl.multiple_of(c * 256, 256), 256)
    loads = [
        pltpu.make_async_copy(src, dst, load_sem.at[i])
        for i, (src, dst) in enumerate(
            [
                (qn_hbm, qn), (qr_hbm, qr), (nlat_hbm, nlat), (nrope_hbm, nrope), (dest_hbm, dest),
                (kup_hbm, kup),
                (rlat_hbm, lat.at[0, :, half, :]), (rrope_hbm, rope.at[0, :, :, half]), (rlen_hbm, rlen),
                (plat_hbm, lat.at[1, :, half, :]), (prope_hbm, rope.at[1, :, :, half]), (plen_hbm, plen),
                (vup_hbm, vup),
            ]
        )
    ]
    need_small, need_kup, need_res, need_inc, need_vup = (
        loads[0:5], loads[5:6], loads[6:9], loads[9:12], loads[12:13]
    )
    for load in loads:
        load.start()
    waiting = list(loads)

    def arrive(wanted):
        for load in wanted:
            load.wait()
            waiting[:] = [other for other in waiting if other is not load]

    sent = []

    def send(copy):
        copy.start()
        sent.append(copy)

    def over_groups(start):
        def step(k, _):
            start((g + k) % NG)
            return 0

        lax.fori_loop(1, NG, step, 0)

    all_sent = []

    def drain():
        for load in waiting:
            load.wait()
        for copy in sent:
            copy.wait_send()
        for copy in all_sent:
            copy.wait_send()

    def remote(src, dst, ss, rs, device):
        return pltpu.make_async_remote_copy(
            src_ref=src, dst_ref=dst, send_sem=ss, recv_sem=rs, device_id=device, device_id_type=MESH
        )

    def sib_copies(p):
        lat_hbm, rope_hbm = ((rlat_hbm, rrope_hbm), (plat_hbm, prope_hbm))[p]
        return (
            remote(lat_hbm, lat.at[p, :, half, :], sib_ss.at[p, 0], sib_rs.at[p, 0], sibling),
            remote(rope_hbm, rope.at[p, :, :, half], sib_ss.at[p, 1], sib_rs.at[p, 1], sibling),
        )

    arrive(need_small)
    qn_all = qn[...].astype(F32).reshape(64, 128)
    qr_all = qr[...].astype(F32).reshape(64, 64)
    fresh_all = nlat[...].astype(F32)
    fresh_rope_all = nrope[...].astype(F32)
    rope_rows = [
        jnp.concatenate([qr_all[s * 16 : s * 16 + 8], qr_all[s * 16 + 8 : s * 16 + 16]], axis=1)
        for s in (2, 3)
    ]
    pay_a[y] = jnp.concatenate([qn_all[32:64]] + rope_rows, axis=0).astype(BF16)
    for i in range(2):
        dest_x[x * 2 + i] = jnp.full((1, 128), dest[0, i].astype(F32))
        dest_all[g * 2 + i] = jnp.full((1, 128), dest[0, i].astype(F32))

    pl.semaphore_wait(barrier, len(peers))

    def ya_copy(to, frm):
        return remote(pay_a.at[y], pay_a.at[y], ya_ss.at[to], ya_rs.at[frm], (x * NY + to, d))

    def yb_copy(to, frm):
        return remote(pay_b.at[y], pay_b.at[y], yb_ss.at[to], yb_rs.at[frm], (x * NY + to, d))

    def dx_copy(to, frm):
        ref = dest_x.at[pl.ds(x * 2, 2)]
        return remote(ref, ref, dx_ss.at[to], dx_rs.at[frm], (to * NY + y, d))

    for k in (4, 3, 5, 2, 6, 1, 7):
        send(ya_copy((y + k) % NY, y))
    for k in range(1, NX):
        send(dx_copy((x + k) % NX, x))

    GATHER = ((0, 1), (0, -1), (0, 2), (0, -2), (-2, 1), (2, -1), (-2, 2), (2, -2))

    def part(p, s, chunk, kind):
        cut = 48 if s == 0 else 32
        ref = gathered.at[p, s, (z + chunk + NZ) % NZ]
        if kind == 6:
            return ref.at[pl.ds(0, cut)]
        if kind == 7:
            return ref.at[pl.ds(cut, 80 - cut)]
        return ref

    def gather_out(p, s, kind):
        chunk, by = GATHER[kind]
        ref = part(p, s, chunk, kind)
        return remote(ref, ref, gz_ss.at[p, s, kind], gz_rs.at[p, s, kind], along_z(by))

    def gather_in(p, s, kind):
        chunk, by = GATHER[kind]
        ref = part(p, s, chunk - by, kind)
        return remote(ref, ref, gz_ss.at[p, s, kind], gz_rs.at[p, s, kind], along_z(-by))

    def gather_start(p, absorbed, ropes):
        blank = jnp.zeros((16, 64), F32)
        for s in range(2):
            for k in range(4):
                gathered[p, s, z, k * 16 : (k + 1) * 16, :] = absorbed[
                    s * 16 : (s + 1) * 16, k * 128 : (k + 1) * 128
                ]
            gathered[p, s, z, 64:80, :] = jnp.concatenate([ropes[s], blank], axis=1).astype(BF16)
            for kind in (2, 3):
                send(gather_out(p, s, kind))
        for s in range(2):
            for kind in (0, 1):
                send(gather_out(p, s, kind))

    def gather_mid(p):
        for s in range(2):
            for kind in (2, 3):
                gather_in(p, s, kind).wait_recv()
                send(gather_out(p, s, kind + 2))
                send(gather_out(p, s, kind + 4))

    def gather_end(p, s):
        for kind in (0, 1, 4, 5, 6, 7):
            gather_in(p, s, kind).wait_recv()

    arrive(need_kup)
    absorbed_res = absorb(qn_all[0:32].astype(BF16), kup)
    ropes_res = [qr_all[0:16], qr_all[16:32]]
    gather_start(0, absorbed_res, ropes_res)
    for copy in sib_copies(0):
        send(copy)

    tokens = []
    for i in range(2):
        for n in range(2):
            for k in range(4):
                small[n * 4 + k : n * 4 + k + 1, :] = fresh_all[2 + i, n : n + 1, k * 128 : (k + 1) * 128]
        tokens.append(small[...])
    for i in range(2):
        row = jnp.concatenate([fresh_rope_all[2 + i, 0:1], fresh_rope_all[2 + i, 1:2]], axis=1)
        tokens.append(jnp.broadcast_to(row, (8, 128)))
    pay_b[y] = jnp.concatenate(tokens, axis=0).astype(BF16)
    for k in range(1, NY):
        send(yb_copy((y + k) % NY, y))
    for copy in sib_copies(1):
        send(copy)

    fresh_res = [[fresh_all[s, n : n + 1] for n in range(2)] for s in range(2)]
    fresh_rope_res = [[fresh_rope_all[s, n : n + 1] for n in range(2)] for s in range(2)]
    scores_res = new_scores(scale, absorbed_res, ropes_res, fresh_res, fresh_rope_res)

    def xa_copy(to, frm):
        return remote(xs_a.at[to], xr_a.at[x], xa_ss.at[to], xa_rs.at[frm], (to * NY + y, d))

    def xb_copy(to, frm):
        return remote(xs_b.at[to], xr_b.at[x], xb_ss.at[to], xb_rs.at[frm], (to * NY + y, d))

    def choose_for(to, held, base, width):
        blocks = []
        for r in range(2):
            wanted = dest_x[to * 2 + r]
            block = jnp.zeros((width, 128), F32)
            for j in range(NY):
                for i in range(2):
                    here = ((x * NY + j) * 2 + i).astype(F32)
                    rows = held[j, base + i * width : base + (i + 1) * width, :]
                    block = jnp.where(jnp.broadcast_to(wanted == here, (width, 128)), rows, block)
            blocks.append(block)
        return blocks

    for k in range(1, NY):
        frm = (y + k) % NY
        ya_copy(frm, frm).wait_recv()
    for k in range(1, NX):
        frm = (x + k) % NX
        dx_copy(frm, frm).wait_recv()
    held = pay_a[...].astype(F32)
    for k in (2, 1, 3, 0):
        to = (x + k) % NX
        block = choose_for(to, held, 0, 16) + choose_for(to, held, 32, 8)
        block = jnp.concatenate(block, axis=0).astype(BF16)
        if k:
            xs_a[to] = block
            send(xa_copy(to, x))
        else:
            xr_a[x] = block
    gather_mid(0)
    for k in range(1, NX):
        frm = (x + k) % NX
        xa_copy(frm, frm).wait_recv()
    block = xr_a[0].astype(F32)
    for j in range(1, NX):
        block = block + xr_a[j].astype(F32)
    ropes_inc = [
        jnp.concatenate([block[32 + 8 * r : 40 + 8 * r, 0:64], block[32 + 8 * r : 40 + 8 * r, 64:128]], axis=0)
        for r in range(2)
    ]
    absorbed_inc = absorb(block[0:32].astype(BF16), kup)
    gather_start(1, absorbed_inc, ropes_inc)

    def out_copy(p, s, to, frm):
        device = (g, to * 2 + c)
        return remote(zs_bf.at[p, s, to], zr_bf.at[p, s, z], zo_ss.at[p, s, to], zo_rs.at[p, s, frm], device)

    def stat_copy(p, to, frm):
        device = (g, to * 2 + c)
        return remote(zs_st.at[p, to], zr_st.at[p, z], zt_ss.at[p, to], zt_rs.at[p, frm], device)

    FAR_FIRST = (4, 3, 5, 2, 6, 1, 7)

    NEAR, REST = (0, 2, 6, 1, 7), (4, 3, 5)

    def partials(p, s, lengths, offsets):
        chunks = [(z + k) % NZ for k in offsets]
        return attend(
            scale, gathered.at[p, s], chunks, lat[p, s], rope[p, s], lengths[0, s], z * 512, zs_bf.at[p, s]
        )

    def share(p, s, offsets):
        for k in offsets:
            if k:
                send(out_copy(p, s, (z + k) % NZ, z))
            else:
                zr_bf[p, s, z] = zs_bf[p, s, z]

    def share_stats(p, offsets, fields):
        rows = rows_of([fields[0][0], fields[1][0], fields[0][1], fields[1][1]])
        for i, k in enumerate(offsets):
            to = (z + k) % NZ
            if k:
                zs_st[p, to] = rows[i]
                send(stat_copy(p, to, z))
            else:
                zr_st[p, z] = rows[i]

    def collect(p):
        for k in FAR_FIRST:
            frm = (z + k) % NZ
            for s in range(2):
                out_copy(p, s, frm, frm).wait_recv()
            stat_copy(p, frm, frm).wait_recv()

    for k in range(1, NY):
        frm = (y + k) % NY
        yb_copy(frm, frm).wait_recv()
    held = pay_b[...].astype(F32)
    for k in (2, 1, 3, 0):
        to = (x + k) % NX
        block = choose_for(to, held, 0, 8) + choose_for(to, held, 16, 8)
        block = jnp.concatenate(block, axis=0).astype(BF16)
        if k:
            xs_b[to] = block
            send(xb_copy(to, x))
        else:
            xr_b[x] = block
    gather_mid(1)
    arrive(need_inc)
    for copy in sib_copies(1):
        copy.wait_recv()
    for offsets, kinds in ((NEAR, (0, 1)), (REST, (4, 5, 6, 7))):
        fields_inc = []
        for s in range(2):
            for kind in kinds:
                gather_in(1, s, kind).wait_recv()
            fields_inc.append(partials(1, s, plen, offsets))
            share(1, s, offsets)
        share_stats(1, offsets, fields_inc)
    arrive(need_res)
    for copy in sib_copies(0):
        copy.wait_recv()
    fields_res = []
    gather_end(0, 0)
    fields_res.append(partials(0, 0, rlen, NEAR + REST))
    gather_end(0, 1)
    fields_res.append(partials(0, 1, rlen, NEAR + REST))
    share(0, 0, REST + NEAR)
    share(0, 1, REST + NEAR)
    share_stats(0, NEAR + REST, fields_res)
    for k in range(1, NX):
        frm = (x + k) % NX
        xb_copy(frm, frm).wait_recv()
    block = xr_b[0].astype(F32)
    for j in range(1, NX):
        block = block + xr_b[j].astype(F32)
    fresh_inc, fresh_rope_inc = [], []
    for r in range(2):
        small[...] = block[8 * r : 8 * r + 8]
        fresh_inc.append(
            [
                jnp.concatenate([small[n * 4 + k : n * 4 + k + 1, :] for k in range(4)], axis=1)
                for n in range(2)
            ]
        )
        row = block[16 + 8 * r : 17 + 8 * r]
        fresh_rope_inc.append([row[:, 0:64], row[:, 64:128]])
    scores_inc = new_scores(scale, absorbed_inc, ropes_inc, fresh_inc, fresh_rope_inc)

    def da_copy(to):
        ref = dest_all.at[pl.ds(g * 2, 2)]
        return remote(ref, ref, da_ss, da_rs, (to, d))

    over_groups(lambda to: da_copy(to).start())
    da_every = remote(dest_all.at[pl.ds(0, 62)], dest_all.at[pl.ds(0, 62)], da_ss, da_rs, along_y(1))
    all_sent.append(da_every)

    arrive(need_vup)
    collect(1)
    out_inc = finish(zr_bf.at[1], zr_st.at[1], scores_inc, fresh_inc, vup)

    def ret_block(to):
        block = jnp.zeros((16, 128), F32)
        for r in range(2):
            goal = dest_all[g * 2 + r]
            first = (to * 2).astype(F32)
            hit = (goal == first) | (goal == first + 1.0)
            block = jnp.where(jnp.broadcast_to(hit, (16, 128)), out_inc[r * 16 : (r + 1) * 16], block)
        return block.astype(BF16)

    def ret_start(to):
        ret_send[to] = ret_block(to)
        remote(ret_send.at[to], ret_recv.at[g], ret_ss, ret_rs, (to, d)).start()

    for ky in FAR_FIRST + (0,):
        for kx in (2, 1, 3, 0):
            if kx or ky:
                ret_start(((x + kx) % NX) * NY + (y + ky) % NY)
    ret_every = remote(ret_send.at[pl.ds(0, 31)], ret_recv.at[pl.ds(0, 31)], ret_ss, ret_rs, along_y(1))
    all_sent.append(ret_every)
    ret_recv[g] = ret_block(g)

    collect(0)
    out_res = finish(zr_bf.at[0], zr_st.at[0], scores_res, fresh_res, vup)
    out[0:2] = out_res.reshape(2, 2, 8, 128).astype(BF16)

    da_every.wait_recv()
    ret_every.wait_recv()

    def choose(frm, chosen):
        block = ret_recv[frm].astype(F32)
        picked = []
        for i in range(2):
            here = (g * 2 + i).astype(F32)
            hit = (dest_all[frm * 2] == here) | (dest_all[frm * 2 + 1] == here)
            picked.append(jnp.where(jnp.broadcast_to(hit, (16, 128)), block, chosen[i]))
        return tuple(picked)

    zero = jnp.zeros((16, 128), F32)
    chosen = lax.fori_loop(0, NG, choose, (zero, zero))
    for i in range(2):
        out[2 + i] = chosen[i].reshape(2, 8, 128).astype(BF16)

    drain()


def body(
    prompt_latent_cache, prompt_rope, prompt_length, dest_slot, resident_latent, resident_rope,
    resident_length, new_latent, new_rope, query_nope, query_rope, key_up, value_up_weight,
):
    scale = attend_scale(query_nope.shape[-1], query_rope.shape[-1])
    hbm = pl.BlockSpec(memory_space=pltpu.HBM)
    dma = pltpu.SemaphoreType.DMA
    vmem = pltpu.VMEM
    return pl.pallas_call(
        functools.partial(kernel, scale),
        out_shape=jax.ShapeDtypeStruct((4, 2, 8, 128), BF16),
        in_specs=[hbm] * 13,
        out_specs=pl.BlockSpec(memory_space=pltpu.VMEM),
        scratch_shapes=[
            vmem((2, 2, 512, 512), BF16),
            vmem((2, 2, 64, 512), BF16),
            pltpu.SMEM((1, 2), jnp.int32),
            pltpu.SMEM((1, 2), jnp.int32),
            pltpu.SMEM((1, 2), jnp.int32),
            vmem((4, 2, 512), BF16),
            vmem((4, 2, 64), BF16),
            vmem((4, 2, 8, 128), BF16),
            vmem((4, 2, 8, 64), BF16),
            vmem((8, 128, 512), BF16),
            vmem((8, 512, 128), BF16),
            vmem((NX * 2, 1, 128), F32),
            vmem((NG * 2, 1, 128), F32),
            vmem((NY, 48, 128), BF16),
            vmem((NY, 32, 128), BF16),
            vmem((NX, 48, 128), BF16),
            vmem((NX, 32, 128), BF16),
            vmem((NX, 48, 128), BF16),
            vmem((NX, 32, 128), BF16),
            vmem((2, 2, NZ, 80, 128), BF16),
            vmem((2, 2, NZ, 16, 512), BF16),
            vmem((2, NZ, 1, 128), F32),
            vmem((2, 2, NZ, 16, 512), BF16),
            vmem((2, NZ, 1, 128), F32),
            vmem((NG, 16, 128), BF16),
            vmem((NG, 16, 128), BF16),
            vmem((8, 128), F32),
            dma((13,)),
            dma((2, 2)), dma((2, 2)),
            dma((NY,)), dma((NY,)), dma((NY,)), dma((NY,)),
            dma((NX,)), dma((NX,)), dma((NX,)), dma((NX,)),
            dma((NX,)), dma((NX,)),
            dma, dma,
            dma((2, 2, 8)), dma((2, 2, 8)),
            dma((2, 2, NZ)), dma((2, 2, NZ)),
            dma((2, NZ)), dma((2, NZ)),
            dma, dma,
        ],
        compiler_params=pltpu.CompilerParams(
            collective_id=0, has_side_effects=True, vmem_limit_bytes=48 << 20
        ),
        name="latent_attend",
    )(*(pltpu.with_memory_space_constraint(a, pltpu.HBM) for a in (
        prompt_latent_cache, prompt_rope, prompt_length, dest_slot, resident_latent, resident_rope,
        resident_length, new_latent, new_rope, query_nope, query_rope, key_up, value_up_weight,
    )))


def solution(mesh):
    placed = (
        P("grp", "dev", None),
        P("grp", None, "dev"),
        P("grp", None),
        P("grp", None),
        P("grp", "dev", None),
        P("grp", None, "dev"),
        P("grp", None),
        P("grp", None, None),
        P("grp", None, None),
        P("grp", None, "dev", None),
        P("grp", None, "dev", None),
        P("dev", None, None),
        P("dev", None, None),
    )
    return jax.shard_map(
        body, mesh=mesh, in_specs=placed, out_specs=P("grp", None, "dev", None), check_vma=False
    )
```

```python
import functools
import math

import jax
import jax.numpy as jnp
from jax import lax
from jax.experimental import pallas as pl
from jax.experimental.pallas import tpu as pltpu
from jax.sharding import PartitionSpec as P

MESH = pl.DeviceIdType.MESH
F32 = jnp.float32
BF16 = jnp.bfloat16
NX, NY, NZ = 4, 8, 8
NG = NX * NY
NEG = -1e30


def attend_scale(nope_width, rotary_width):
    return (0.1 * math.log(40.0) + 1.0) ** 2 / math.sqrt(nope_width + rotary_width)


def iota(shape, axis):
    return lax.broadcasted_iota(jnp.int32, shape, axis)


def columns_of(rows, field):
    n = rows.shape[0]
    hit = iota((n, 16, 128), 2) == iota((n, 16, 128), 1) + 16 * field
    return jnp.sum(jnp.where(hit, jnp.broadcast_to(rows, (n, 16, 128)), 0.0), axis=-1, keepdims=True)


def rows_of(fields):
    n = fields[0].shape[0]
    lane, sub = iota((n, 16, 128), 2), iota((n, 16, 128), 1)
    packed = jnp.zeros((n, 16, 128), F32)
    for f, column in enumerate(fields):
        packed = jnp.where(lane == sub + 16 * f, jnp.broadcast_to(column, (n, 16, 128)), packed)
    return jnp.sum(packed, axis=1, keepdims=True)


def absorb(q32, kup):
    head = iota((32, 512), 0) % 8
    total = jnp.zeros((32, 512), F32)
    for h in range(8):
        total = jnp.where(head == h, jnp.dot(q32, kup[h], preferred_element_type=F32), total)
    return total.astype(BF16)


def new_scores(scale, absorbed, ropes, fresh, fresh_rope):
    step = iota((16, 1), 0) // 8
    out = []
    for s in range(2):
        q = absorbed[s * 16 : (s + 1) * 16].astype(F32)
        pair = []
        for n in range(2):
            v = jnp.sum(q * fresh[s][n], axis=-1, keepdims=True)
            v = v + jnp.sum(ropes[s] * fresh_rope[s][n], axis=-1, keepdims=True)
            v = v * scale
            pair.append(v if n == 0 else jnp.where(step >= 1, v, NEG))
        out.append(pair)
    return out


def attend(scale, gathered, chunks, keys, rope, length, offset, out_bf):
    n = len(chunks)
    rows = [gathered[chunk] for chunk in chunks]
    q = jnp.concatenate(
        [jnp.concatenate([r[k * 16 : (k + 1) * 16] for r in rows], axis=0) for k in range(4)], axis=1
    )
    ropes = jnp.concatenate([r[64:80] for r in rows], axis=0)[:, 0:64]
    scores = lax.dot_general(q, keys, (((1,), (1,)), ((), ())), preferred_element_type=F32)
    scores = scale * (scores + jnp.dot(ropes, rope, preferred_element_type=F32))
    live = offset + iota((n * 16, 512), 1) < length
    scores = jnp.where(live, scores, NEG)
    top = jnp.max(scores, axis=-1, keepdims=True)
    weights = jnp.where(live, jnp.exp(scores - top), 0.0)
    total = jnp.sum(weights, axis=-1, keepdims=True)
    summed = jnp.dot(weights.astype(BF16), keys, preferred_element_type=F32)
    summed = (summed / jnp.maximum(total, 1.0)).astype(BF16)
    for i, chunk in enumerate(chunks):
        out_bf[chunk] = summed[i * 16 : (i + 1) * 16]
    return top.reshape(n, 16, 1), total.reshape(n, 16, 1)


def finish(blocks, stats, fresh_scores, fresh, vup):
    rows = []
    for s in range(2):
        m, l = columns_of(stats[...], s), columns_of(stats[...], 2 + s)
        n0, n1 = fresh_scores[s]
        top = jnp.maximum(jnp.max(m, axis=0), jnp.maximum(n0, n1))
        w = l * jnp.exp(m - top[None])
        w0 = jnp.exp(n0 - top)
        w1 = jnp.where(n1 > NEG, jnp.exp(n1 - top), 0.0)
        under = jnp.sum(w, axis=0) + w0 + w1
        total = w0 * fresh[s][0] + w1 * fresh[s][1]
        for j in range(NZ):
            total = total + w[j] * blocks[s, j].astype(F32)
        rows.append(total / under)
    attended = jnp.concatenate(rows, axis=0).astype(BF16)
    head = iota((32, 128), 0) % 8
    out = jnp.zeros((32, 128), F32)
    for h in range(8):
        out = jnp.where(head == h, jnp.dot(attended, vup[h], preferred_element_type=F32), out)
    return out


def kernel(
    scale,
    plat_hbm, prope_hbm, plen_hbm, dest_hbm, rlat_hbm, rrope_hbm, rlen_hbm, nlat_hbm, nrope_hbm,
    qn_hbm, qr_hbm, kup_hbm, vup_hbm,
    out,
    lat, rope, plen, dest, rlen, nlat, nrope, qn, qr, kup, vup,
    dest_x, dest_all, pay_a, pay_b, xs_a, xs_b, xr_a, xr_b, gathered,
    zs_bf, zs_st, zr_bf, zr_st, ret_send, ret_recv, small,
    load_sem, sib_ss, sib_rs, ya_ss, ya_rs, yb_ss, yb_rs, xa_ss, xa_rs, xb_ss, xb_rs,
    dx_ss, dx_rs, da_ss, da_rs, gz_ss, gz_rs, zo_ss, zo_rs, zt_ss, zt_rs, ret_ss, ret_rs,
):
    g, d = lax.axis_index("grp"), lax.axis_index("dev")
    x, y = g // NY, g % NY
    z, c = d // 2, d % 2

    def along_z(k):
        return (g, ((z + k + NZ) % NZ) * 2 + c)

    def along_y(k):
        return (x * NY + (y + k) % NY, d)

    def along_x(k):
        return (((x + k) % NX) * NY + y, d)

    sibling = (g, z * 2 + 1 - c)

    barrier = pltpu.get_barrier_semaphore()
    peers = [along_y(k) for k in (4, 3, 5, 2, 6)] + [along_x(2)] + [along_z(k) for k in (2, -2)]
    peers += [along_y(k) for k in (1, 7)] + [along_x(k) for k in (1, 3)] + [along_z(k) for k in (1, -1)] + [sibling]
    for peer in peers:
        pl.semaphore_signal(barrier, inc=1, device_id=peer, device_id_type=MESH)

    half = pl.ds(pl.multiple_of(c * 256, 256), 256)
    loads = [
        pltpu.make_async_copy(src, dst, load_sem.at[i])
        for i, (src, dst) in enumerate(
            [
                (qn_hbm, qn), (qr_hbm, qr), (nlat_hbm, nlat), (nrope_hbm, nrope), (dest_hbm, dest),
                (kup_hbm, kup),
                (rlat_hbm, lat.at[0, :, half, :]), (rrope_hbm, rope.at[0, :, :, half]), (rlen_hbm, rlen),
                (plat_hbm, lat.at[1, :, half, :]), (prope_hbm, rope.at[1, :, :, half]), (plen_hbm, plen),
                (vup_hbm, vup),
            ]
        )
    ]
    need_small, need_kup, need_res, need_inc, need_vup = (
        loads[0:5], loads[5:6], loads[6:9], loads[9:12], loads[12:13]
    )
    for load in loads:
        load.start()
    waiting = list(loads)

    def arrive(wanted):
        for load in wanted:
            load.wait()
            waiting[:] = [other for other in waiting if other is not load]

    sent = []

    def send(copy):
        copy.start()
        sent.append(copy)

    def over_groups(start):
        def step(k, _):
            start((g + k) % NG)
            return 0

        lax.fori_loop(1, NG, step, 0)

    all_sent = []

    def drain():
        for load in waiting:
            load.wait()
        for copy in sent:
            copy.wait_send()
        for copy in all_sent:
            copy.wait_send()

    def remote(src, dst, ss, rs, device):
        return pltpu.make_async_remote_copy(
            src_ref=src, dst_ref=dst, send_sem=ss, recv_sem=rs, device_id=device, device_id_type=MESH
        )

    def sib_copies(p):
        lat_hbm, rope_hbm = ((rlat_hbm, rrope_hbm), (plat_hbm, prope_hbm))[p]
        return (
            remote(lat_hbm, lat.at[p, :, half, :], sib_ss.at[p, 0], sib_rs.at[p, 0], sibling),
            remote(rope_hbm, rope.at[p, :, :, half], sib_ss.at[p, 1], sib_rs.at[p, 1], sibling),
        )

    arrive(need_small)
    qn_all = qn[...].astype(F32).reshape(64, 128)
    qr_all = qr[...].astype(F32).reshape(64, 64)
    fresh_all = nlat[...].astype(F32)
    fresh_rope_all = nrope[...].astype(F32)
    rope_rows = [
        jnp.concatenate([qr_all[s * 16 : s * 16 + 8], qr_all[s * 16 + 8 : s * 16 + 16]], axis=1)
        for s in (2, 3)
    ]
    pay_a[y] = jnp.concatenate([qn_all[32:64]] + rope_rows, axis=0).astype(BF16)
    for i in range(2):
        dest_x[x * 2 + i] = jnp.full((1, 128), dest[0, i].astype(F32))
        dest_all[g * 2 + i] = jnp.full((1, 128), dest[0, i].astype(F32))

    pl.semaphore_wait(barrier, len(peers))

    def ya_copy(to, frm):
        return remote(pay_a.at[y], pay_a.at[y], ya_ss.at[to], ya_rs.at[frm], (x * NY + to, d))

    def yb_copy(to, frm):
        return remote(pay_b.at[y], pay_b.at[y], yb_ss.at[to], yb_rs.at[frm], (x * NY + to, d))

    def dx_copy(to, frm):
        ref = dest_x.at[pl.ds(x * 2, 2)]
        return remote(ref, ref, dx_ss.at[to], dx_rs.at[frm], (to * NY + y, d))

    for k in (4, 3, 5, 2, 6, 1, 7):
        send(ya_copy((y + k) % NY, y))
    for k in range(1, NX):
        send(dx_copy((x + k) % NX, x))

    GATHER = ((0, 1), (0, -1), (0, 2), (0, -2), (-2, 1), (2, -1), (-2, 2), (2, -2))

    def part(p, s, chunk, kind):
        cut = 48 if s == 0 else 32
        ref = gathered.at[p, s, (z + chunk + NZ) % NZ]
        if kind == 6:
            return ref.at[pl.ds(0, cut)]
        if kind == 7:
            return ref.at[pl.ds(cut, 80 - cut)]
        return ref

    def gather_out(p, s, kind):
        chunk, by = GATHER[kind]
        ref = part(p, s, chunk, kind)
        return remote(ref, ref, gz_ss.at[p, s, kind], gz_rs.at[p, s, kind], along_z(by))

    def gather_in(p, s, kind):
        chunk, by = GATHER[kind]
        ref = part(p, s, chunk - by, kind)
        return remote(ref, ref, gz_ss.at[p, s, kind], gz_rs.at[p, s, kind], along_z(-by))

    def gather_start(p, absorbed, ropes):
        blank = jnp.zeros((16, 64), F32)
        for s in range(2):
            for k in range(4):
                gathered[p, s, z, k * 16 : (k + 1) * 16, :] = absorbed[
                    s * 16 : (s + 1) * 16, k * 128 : (k + 1) * 128
                ]
            gathered[p, s, z, 64:80, :] = jnp.concatenate([ropes[s], blank], axis=1).astype(BF16)
            for kind in (2, 3):
                send(gather_out(p, s, kind))
        for s in range(2):
            for kind in (0, 1):
                send(gather_out(p, s, kind))

    def gather_mid(p):
        for s in range(2):
            for kind in (2, 3):
                gather_in(p, s, kind).wait_recv()
                send(gather_out(p, s, kind + 2))
                send(gather_out(p, s, kind + 4))

    def gather_end(p, s):
        for kind in (0, 1, 4, 5, 6, 7):
            gather_in(p, s, kind).wait_recv()

    arrive(need_kup)
    absorbed_res = absorb(qn_all[0:32].astype(BF16), kup)
    ropes_res = [qr_all[0:16], qr_all[16:32]]
    gather_start(0, absorbed_res, ropes_res)
    for copy in sib_copies(0):
        send(copy)

    tokens = []
    for i in range(2):
        for n in range(2):
            for k in range(4):
                small[n * 4 + k : n * 4 + k + 1, :] = fresh_all[2 + i, n : n + 1, k * 128 : (k + 1) * 128]
        tokens.append(small[...])
    for i in range(2):
        row = jnp.concatenate([fresh_rope_all[2 + i, 0:1], fresh_rope_all[2 + i, 1:2]], axis=1)
        tokens.append(jnp.broadcast_to(row, (8, 128)))
    pay_b[y] = jnp.concatenate(tokens, axis=0).astype(BF16)
    for k in range(1, NY):
        send(yb_copy((y + k) % NY, y))
    for copy in sib_copies(1):
        send(copy)

    fresh_res = [[fresh_all[s, n : n + 1] for n in range(2)] for s in range(2)]
    fresh_rope_res = [[fresh_rope_all[s, n : n + 1] for n in range(2)] for s in range(2)]
    scores_res = new_scores(scale, absorbed_res, ropes_res, fresh_res, fresh_rope_res)

    def xa_copy(to, frm):
        return remote(xs_a.at[to], xr_a.at[x], xa_ss.at[to], xa_rs.at[frm], (to * NY + y, d))

    def xb_copy(to, frm):
        return remote(xs_b.at[to], xr_b.at[x], xb_ss.at[to], xb_rs.at[frm], (to * NY + y, d))

    def choose_for(to, held, base, width):
        blocks = []
        for r in range(2):
            wanted = dest_x[to * 2 + r]
            block = jnp.zeros((width, 128), F32)
            for j in range(NY):
                for i in range(2):
                    here = ((x * NY + j) * 2 + i).astype(F32)
                    rows = held[j, base + i * width : base + (i + 1) * width, :]
                    block = jnp.where(jnp.broadcast_to(wanted == here, (width, 128)), rows, block)
            blocks.append(block)
        return blocks

    for k in range(1, NY):
        frm = (y + k) % NY
        ya_copy(frm, frm).wait_recv()
    for k in range(1, NX):
        frm = (x + k) % NX
        dx_copy(frm, frm).wait_recv()
    held = pay_a[...].astype(F32)
    for k in (2, 1, 3, 0):
        to = (x + k) % NX
        block = choose_for(to, held, 0, 16) + choose_for(to, held, 32, 8)
        block = jnp.concatenate(block, axis=0).astype(BF16)
        if k:
            xs_a[to] = block
            send(xa_copy(to, x))
        else:
            xr_a[x] = block
    gather_mid(0)
    for k in range(1, NX):
        frm = (x + k) % NX
        xa_copy(frm, frm).wait_recv()
    block = xr_a[0].astype(F32)
    for j in range(1, NX):
        block = block + xr_a[j].astype(F32)
    ropes_inc = [
        jnp.concatenate([block[32 + 8 * r : 40 + 8 * r, 0:64], block[32 + 8 * r : 40 + 8 * r, 64:128]], axis=0)
        for r in range(2)
    ]
    absorbed_inc = absorb(block[0:32].astype(BF16), kup)
    gather_start(1, absorbed_inc, ropes_inc)

    def out_copy(p, s, to, frm):
        device = (g, to * 2 + c)
        return remote(zs_bf.at[p, s, to], zr_bf.at[p, s, z], zo_ss.at[p, s, to], zo_rs.at[p, s, frm], device)

    def stat_copy(p, to, frm):
        device = (g, to * 2 + c)
        return remote(zs_st.at[p, to], zr_st.at[p, z], zt_ss.at[p, to], zt_rs.at[p, frm], device)

    FAR_FIRST = (4, 3, 5, 2, 6, 1, 7)

    NEAR, REST = (0, 2, 6, 1, 7), (4, 3, 5)

    def partials(p, s, lengths, offsets):
        chunks = [(z + k) % NZ for k in offsets]
        return attend(
            scale, gathered.at[p, s], chunks, lat[p, s], rope[p, s], lengths[0, s], z * 512, zs_bf.at[p, s]
        )

    def share(p, s, offsets):
        for k in offsets:
            if k:
                send(out_copy(p, s, (z + k) % NZ, z))
            else:
                zr_bf[p, s, z] = zs_bf[p, s, z]

    def share_stats(p, offsets, fields):
        rows = rows_of([fields[0][0], fields[1][0], fields[0][1], fields[1][1]])
        for i, k in enumerate(offsets):
            to = (z + k) % NZ
            if k:
                zs_st[p, to] = rows[i]
                send(stat_copy(p, to, z))
            else:
                zr_st[p, z] = rows[i]

    def collect(p):
        for k in FAR_FIRST:
            frm = (z + k) % NZ
            for s in range(2):
                out_copy(p, s, frm, frm).wait_recv()
            stat_copy(p, frm, frm).wait_recv()

    for k in range(1, NY):
        frm = (y + k) % NY
        yb_copy(frm, frm).wait_recv()
    held = pay_b[...].astype(F32)
    for k in (2, 1, 3, 0):
        to = (x + k) % NX
        block = choose_for(to, held, 0, 8) + choose_for(to, held, 16, 8)
        block = jnp.concatenate(block, axis=0).astype(BF16)
        if k:
            xs_b[to] = block
            send(xb_copy(to, x))
        else:
            xr_b[x] = block
    gather_mid(1)
    arrive(need_inc)
    for copy in sib_copies(1):
        copy.wait_recv()
    for offsets, kinds in ((NEAR, (0, 1)), (REST, (4, 5, 6, 7))):
        fields_inc = []
        for s in range(2):
            for kind in kinds:
                gather_in(1, s, kind).wait_recv()
            fields_inc.append(partials(1, s, plen, offsets))
            share(1, s, offsets)
        share_stats(1, offsets, fields_inc)
    arrive(need_res)
    for copy in sib_copies(0):
        copy.wait_recv()
    fields_res = []
    gather_end(0, 0)
    fields_res.append(partials(0, 0, rlen, NEAR + REST))
    gather_end(0, 1)
    fields_res.append(partials(0, 1, rlen, NEAR + REST))
    share(0, 0, REST + NEAR)
    share(0, 1, REST + NEAR)
    share_stats(0, NEAR + REST, fields_res)
    for k in range(1, NX):
        frm = (x + k) % NX
        xb_copy(frm, frm).wait_recv()
    block = xr_b[0].astype(F32)
    for j in range(1, NX):
        block = block + xr_b[j].astype(F32)
    fresh_inc, fresh_rope_inc = [], []
    for r in range(2):
        small[...] = block[8 * r : 8 * r + 8]
        fresh_inc.append(
            [
                jnp.concatenate([small[n * 4 + k : n * 4 + k + 1, :] for k in range(4)], axis=1)
                for n in range(2)
            ]
        )
        row = block[16 + 8 * r : 17 + 8 * r]
        fresh_rope_inc.append([row[:, 0:64], row[:, 64:128]])
    scores_inc = new_scores(scale, absorbed_inc, ropes_inc, fresh_inc, fresh_rope_inc)

    def da_copy(to):
        ref = dest_all.at[pl.ds(g * 2, 2)]
        return remote(ref, ref, da_ss, da_rs, (to, d))

    over_groups(lambda to: da_copy(to).start())
    da_every = remote(dest_all.at[pl.ds(0, 62)], dest_all.at[pl.ds(0, 62)], da_ss, da_rs, along_y(1))
    all_sent.append(da_every)

    arrive(need_vup)
    collect(1)
    out_inc = finish(zr_bf.at[1], zr_st.at[1], scores_inc, fresh_inc, vup)

    def ret_block(to):
        block = jnp.zeros((16, 128), F32)
        for r in range(2):
            goal = dest_all[g * 2 + r]
            first = (to * 2).astype(F32)
            hit = (goal == first) | (goal == first + 1.0)
            block = jnp.where(jnp.broadcast_to(hit, (16, 128)), out_inc[r * 16 : (r + 1) * 16], block)
        return block.astype(BF16)

    def ret_start(to):
        ret_send[to] = ret_block(to)
        remote(ret_send.at[to], ret_recv.at[g], ret_ss, ret_rs, (to, d)).start()

    for ky in FAR_FIRST + (0,):
        for kx in (2, 1, 3, 0):
            if kx or ky:
                ret_start(((x + kx) % NX) * NY + (y + ky) % NY)
    ret_every = remote(ret_send.at[pl.ds(0, 31)], ret_recv.at[pl.ds(0, 31)], ret_ss, ret_rs, along_y(1))
    all_sent.append(ret_every)
    ret_recv[g] = ret_block(g)

    collect(0)
    out_res = finish(zr_bf.at[0], zr_st.at[0], scores_res, fresh_res, vup)
    out[0:2] = out_res.reshape(2, 2, 8, 128).astype(BF16)

    da_every.wait_recv()
    ret_every.wait_recv()

    def choose(frm, chosen):
        block = ret_recv[frm].astype(F32)
        picked = []
        for i in range(2):
            here = (g * 2 + i).astype(F32)
            hit = (dest_all[frm * 2] == here) | (dest_all[frm * 2 + 1] == here)
            picked.append(jnp.where(jnp.broadcast_to(hit, (16, 128)), block, chosen[i]))
        return tuple(picked)

    zero = jnp.zeros((16, 128), F32)
    chosen = lax.fori_loop(0, NG, choose, (zero, zero))
    for i in range(2):
        out[2 + i] = chosen[i].reshape(2, 8, 128).astype(BF16)

    drain()


def body(
    prompt_latent_cache, prompt_rope, prompt_length, dest_slot, resident_latent, resident_rope,
    resident_length, new_latent, new_rope, query_nope, query_rope, key_up, value_up_weight,
):
    scale = attend_scale(query_nope.shape[-1], query_rope.shape[-1])
    hbm = pl.BlockSpec(memory_space=pltpu.HBM)
    dma = pltpu.SemaphoreType.DMA
    vmem = pltpu.VMEM
    return pl.pallas_call(
        functools.partial(kernel, scale),
        out_shape=jax.ShapeDtypeStruct((4, 2, 8, 128), BF16),
        in_specs=[hbm] * 13,
        out_specs=pl.BlockSpec(memory_space=pltpu.VMEM),
        scratch_shapes=[
            vmem((2, 2, 512, 512), BF16),
            vmem((2, 2, 64, 512), BF16),
            pltpu.SMEM((1, 2), jnp.int32),
            pltpu.SMEM((1, 2), jnp.int32),
            pltpu.SMEM((1, 2), jnp.int32),
            vmem((4, 2, 512), BF16),
            vmem((4, 2, 64), BF16),
            vmem((4, 2, 8, 128), BF16),
            vmem((4, 2, 8, 64), BF16),
            vmem((8, 128, 512), BF16),
            vmem((8, 512, 128), BF16),
            vmem((NX * 2, 1, 128), F32),
            vmem((NG * 2, 1, 128), F32),
            vmem((NY, 48, 128), BF16),
            vmem((NY, 32, 128), BF16),
            vmem((NX, 48, 128), BF16),
            vmem((NX, 32, 128), BF16),
            vmem((NX, 48, 128), BF16),
            vmem((NX, 32, 128), BF16),
            vmem((2, 2, NZ, 80, 128), BF16),
            vmem((2, 2, NZ, 16, 512), BF16),
            vmem((2, NZ, 1, 128), F32),
            vmem((2, 2, NZ, 16, 512), BF16),
            vmem((2, NZ, 1, 128), F32),
            vmem((NG, 16, 128), BF16),
            vmem((NG, 16, 128), BF16),
            vmem((8, 128), F32),
            dma((13,)),
            dma((2, 2)), dma((2, 2)),
            dma((NY,)), dma((NY,)), dma((NY,)), dma((NY,)),
            dma((NX,)), dma((NX,)), dma((NX,)), dma((NX,)),
            dma((NX,)), dma((NX,)),
            dma, dma,
            dma((2, 2, 8)), dma((2, 2, 8)),
            dma((2, 2, NZ)), dma((2, 2, NZ)),
            dma((2, NZ)), dma((2, NZ)),
            dma, dma,
        ],
        compiler_params=pltpu.CompilerParams(
            collective_id=0, has_side_effects=True, vmem_limit_bytes=48 << 20
        ),
        name="latent_attend",
    )(*(pltpu.with_memory_space_constraint(a, pltpu.HBM) for a in (
        prompt_latent_cache, prompt_rope, prompt_length, dest_slot, resident_latent, resident_rope,
        resident_length, new_latent, new_rope, query_nope, query_rope, key_up, value_up_weight,
    )))


def solution(mesh):
    placed = (
        P("grp", "dev", None),
        P("grp", None, "dev"),
        P("grp", None),
        P("grp", None),
        P("grp", "dev", None),
        P("grp", None, "dev"),
        P("grp", None),
        P("grp", None, None),
        P("grp", None, None),
        P("grp", None, "dev", None),
        P("grp", None, "dev", None),
        P("dev", None, None),
        P("dev", None, None),
    )
    return jax.shard_map(
        body, mesh=mesh, in_specs=placed, out_specs=P("grp", None, "dev", None), check_vma=False
    )
```
